1024 devices in a mesh: row: 16 (over z_lo), col: 8 (over y, core), layer: 8 (over z_hi, x).
Axes of the slice: x: 4, y: 4, z: 32 (z_hi: 2, z_lo: 16; z = z_hi * 16 + z_lo), core: 2. Of those that a mesh axis runs over, the one named last changes fastest.
Arguments:
- density: bfloat16 [6144, 6144], P('row', 'col'), may hold values from -0.5 to 0.5
- occupancy: int32 [48, 48], replicated, may hold values from 0 to 1, as said below
Outputs:
- purified: float32 [6144, 6144], P(('row', 'layer'), 'col')
The draws below stay inside these ranges and needn't reach their ends.
Inputs may be any that keep to these rules, and one draw needn't show every extreme that they name: `occupancy`: block (i, j) is occupied wherever |i - j| <= 8; other blocks may or may not be.
All inputs are finite; a program needn't handle non-finite values.
Results may differ from the reference program's by a relative error of at most 0.0029.
Values may be sent and summed in bfloat16 or wider, within the bound.
A program may use at most 32 MiB of HBM per device.

```python
import jax
import jax.numpy as jnp

BS = 128
NB = 48
ORDER = 6144


def draw_occupancy(key, part):
    key = jax.random.fold_in(key, 7)
    scatter_key = jax.random.fold_in(key, 1)
    column_key = jax.random.fold_in(key, 2)
    scattered = (jax.random.randint(scatter_key, (NB, NB), 0, 1000) < 80).astype(jnp.int32)
    row_ids = jnp.arange(NB, dtype=jnp.int32)[:, None]
    column_ids = jnp.arange(NB, dtype=jnp.int32)[None, :]
    banded = (jnp.abs(row_ids - column_ids) <= max(1, NB // 6)).astype(jnp.int32)
    chosen = jax.random.randint(column_key, (NB, 2), 0, NB)
    picked = jnp.max((column_ids[:, None, :] == chosen[:, :, None]).astype(jnp.int32), axis=1)
    return jnp.maximum(jnp.maximum(scattered, banded), picked)


def steps_of(rng, extent, split, least, top_value):
    def one(position, parts):
        steps = jax.random.uniform(jax.random.fold_in(jax.random.fold_in(rng, 6), position), (parts,), jnp.float32, least / len(split), top_value / len(split))
        return jnp.repeat(jnp.exp(steps), extent[position] // parts).reshape((-1,) + (1,) * (len(extent) - position - 1))

    loudness = one(*split[0])
    for cut in split[1:]:
        loudness = loudness * one(*cut)
    return loudness


def scatter_about(rng, dims, scale, most, shards=(), held_as=jnp.bfloat16):
    values = scale * jax.random.normal(rng, dims, jnp.float32)
    if shards:
        values = values * steps_of(rng, dims, shards, -0.22, 0.18)
    return jnp.clip(values, -most, most).astype(held_as)


def setup_inputs(seed: int = 0) -> dict:
    seeds = jax.random.split(jax.random.key(seed), 3)
    return {
        "density": scatter_about(seeds[0], (ORDER, ORDER), (0.08 * min(2, 6144 // ORDER)), 0.5, ((0, 16), (1, 8))),
        "occupancy": draw_occupancy(jax.random.fold_in(seeds[2], 71), 0),
    }


def spread(occupied, block_size):
    row_blocks, column_blocks = occupied.shape
    widened = jnp.broadcast_to(occupied[:, None, :, None], (row_blocks, block_size, column_blocks, block_size))
    return widened.reshape(row_blocks * block_size, column_blocks * block_size)


def reference(density, occupancy):
    pattern = spread(occupancy.astype(jnp.bfloat16), BS)
    masked = density * pattern
    pattern_wide = pattern.astype(jnp.float32)
    square = (jnp.dot(masked, masked, preferred_element_type=jnp.float32) * pattern_wide).astype(jnp.bfloat16)
    cube = jnp.dot(masked, square, preferred_element_type=jnp.float32) * pattern_wide
    return 3.0 * square.astype(jnp.float32) - 2.0 * cube
```

```python
import jax
import jax.numpy as jnp
from jax import lax
from jax.experimental import pallas as pl
from jax.experimental.pallas import tpu as pltpu
from jax.sharding import PartitionSpec as P

MESH = pl.DeviceIdType.MESH
BS = 128
NC = 3
F32 = jnp.float32
BF16 = jnp.bfloat16


def kernel(density, occupancy, out, tile, left, right1, right2, part1, got1, square, square_got, part2, got2,
           final, final_got, slab_mask, out_mask,
           a1_s, a1_r, a2_s, a2_r, seed_s, seed_r, ring_s, ring_r, sib_s, sib_r,
           r1_s, r1_r, sq_s, sq_r, r2_s, r2_r, f_s, f_r):
    row, col, layer = (lax.axis_index(name) for name in ("row", "col", "layer"))
    group, zi = row // 4, row % 4
    y, core = col // 2, col % 2
    zh, x = layer // 4, layer % 4
    place = 4 * zh + group
    kind = (x + zi) % 4
    rights = (right1, right2)

    def device(x_=x, y_=y, core_=core, place_=place, zi_=zi):
        return {"row": 4 * (place_ % 4) + zi_, "col": 2 * y_ + core_, "layer": 4 * (place_ // 4) + x_}

    sibling = device(core_=1 - core)
    up, down = device(place_=(place + 1) % 8), device(place_=(place + 7) % 8)

    barrier = pltpu.get_barrier_semaphore()
    friends = [sibling, up, down]
    for step in range(1, 4):
        friends.append(device(y_=(y + step) % 4))
        for other in range(2):
            friends.append(device(zi_=(zi + step) % 4, core_=other))
            friends.append(device(x_=(x + step) % 4, core_=other))
    for friend in friends:
        pl.semaphore_signal(barrier, inc=1, device_id=friend, device_id_type=MESH)

    pattern = occupancy[...].astype(F32).astype(BF16)
    blocks = pattern.shape[0]

    def mask(row0, rows, col0, cols):
        row_block = (row0 + lax.broadcasted_iota(jnp.int32, (rows, blocks), 0)) // BS
        rows_hot = (row_block == lax.broadcasted_iota(jnp.int32, (rows, blocks), 1)).astype(F32).astype(BF16)
        col_block = (col0 + lax.broadcasted_iota(jnp.int32, (blocks, cols), 1)) // BS
        cols_hot = (col_block == lax.broadcasted_iota(jnp.int32, (blocks, cols), 0)).astype(F32).astype(BF16)
        chosen = jnp.dot(rows_hot, pattern, preferred_element_type=F32).astype(BF16)
        return jnp.dot(chosen, cols_hot, preferred_element_type=F32)

    tile[...] = density[...] * mask(384 * row, 384, 768 * col, 768).astype(BF16)
    pl.semaphore_wait(barrier, len(friends))

    pending = []

    def send(src, dst, send_sem, recv_sem, target, here=None, only=None):
        copy = pltpu.make_async_remote_copy(
            src_ref=src, dst_ref=dst, send_sem=send_sem, recv_sem=recv_sem, device_id=target, device_id_type=MESH
        )
        if here is None:
            go = only
        else:
            go = jnp.logical_not(here) if only is None else jnp.logical_and(only, jnp.logical_not(here))

            @pl.when(here if only is None else jnp.logical_and(only, here))
            def _():
                pltpu.make_async_copy(src, dst, recv_sem).start()

        if go is None:
            copy.start()
        else:
            pl.when(go)(copy.start)
        pending.append((copy, go))

    def arrive(dst, recv_sem):
        pltpu.make_async_remote_copy(
            src_ref=dst, dst_ref=dst, send_sem=recv_sem, recv_sem=recv_sem, device_id=sibling, device_id_type=MESH
        ).wait_recv()

    seed_zi = (zi + 4 - x) % 4
    for c in range(NC):
        for other in range(2):
            send(
                tile.at[pl.ds(pl.multiple_of(192 * zh + 96 * other, 32), 96),
                        pl.ds(pl.multiple_of(384 * (seed_zi % 2) + BS * c, BS), BS)],
                right1.at[c, pl.ds(pl.multiple_of(192 * (2 * group + zh) + 96 * other, 32), 96)],
                seed_s.at[2 * c + other], seed_r.at[c], device(zi_=seed_zi, core_=other),
                here=jnp.logical_and(seed_zi == zi, core == other), only=core == seed_zi // 2,
            )
    for h in range(2):
        to_zi = (2 * core + h + 4 - x) % 4
        send(
            tile.at[pl.ds(pl.multiple_of(192 * zh, 64), 192), pl.ds(384 * h, 384)],
            left.at[y, pl.ds(pl.multiple_of(192 * (zi % 2), 64), 192)],
            a1_s.at[h], a1_r.at[zi % 2], device(zi_=to_zi, core_=zi // 2),
            here=jnp.logical_and(to_zi == zi, zi // 2 == core),
        )

    def rows_of(place_, core_):
        return pl.multiple_of(192 * (2 * (place_ % 4) + place_ // 4) + 96 * core_, 32)

    def ring_piece(way, hop, core_):
        at = rows_of((place + (8 - hop if way == 0 else hop)) % 8, core_)
        if hop < 4:
            return pl.ds(at, 96)
        return pl.ds(pl.multiple_of(at + 48 * way, 16), 48)

    def ring_send(q, c, way, hop):
        rows = ring_piece(way, hop - 1, core)
        if hop == 4:
            rows = pl.ds(pl.multiple_of(rows.start + 48 * way, 16), 48)
        ref = rights[q].at[c, rows]
        n = ((q * NC + c) * 2 + way) * 4 + hop - 1
        send(ref, ref, ring_s.at[n], ring_r.at[n], up if way == 0 else down)

    def share(q, c, way, hop):
        ref = rights[q].at[c, ring_piece(way, hop, core)]
        n = (q * NC + c) * 9 + (0 if hop == 0 else 1 + 4 * way + hop - 1)
        send(ref, ref, sib_s.at[n], sib_r.at[n], sibling)

    def ring_open(q, c):
        ring_send(q, c, 0, 1)
        ring_send(q, c, 1, 1)
        share(q, c, 0, 0)

    def ring_hop(q, c, hop):
        for way in range(2):
            n = ((q * NC + c) * 2 + way) * 4 + hop - 1
            arrive(rights[q].at[c, ring_piece(way, hop, core)], ring_r.at[n])
            if hop < 4:
                ring_send(q, c, way, hop + 1)
            share(q, c, way, hop)

    def ring_close(q, c):
        for way, hop in [(0, 0)] + [(way, hop) for hop in range(1, 5) for way in range(2)]:
            n = (q * NC + c) * 9 + (0 if hop == 0 else 1 + 4 * way + hop - 1)
            arrive(rights[q].at[c, ring_piece(way, hop, 1 - core)], sib_r.at[n])

    def product(q, c):
        total = jnp.dot(left[0], rights[q][c, pl.ds(0, 384)], preferred_element_type=F32)
        for j in range(1, 4):
            total += jnp.dot(left[j], rights[q][c, pl.ds(384 * j, 384)], preferred_element_type=F32)
        return total

    own_rows = rows_of(place, core)

    for c in range(NC):
        arrive(right1.at[c, pl.ds(own_rows, 96)], seed_r.at[c])
        ring_open(0, c)
    for h in range(2):
        arrive(left.at[y, pl.ds(192 * h, 192)], a1_r.at[h])
    for step in range(1, 4):
        send(left.at[y], left.at[y], a2_s.at[step - 1], a2_r.at[step - 1], device(y_=(y + step) % 4))

    slab_mask[...] = mask(384 * (4 * group + kind) + 192 * zh + 96 * core, 96, 1536 * y + 384 * zi, 384)
    for h in range(2):
        out_mask[h] = mask(384 * (4 * group + 2 * core + h) + 192 * zh + 48 * x, 48, 1536 * y + 384 * zi, 384)

    for hop in range(1, 5):
        for c in range(NC):
            ring_hop(0, c, hop)
    for step in range(1, 4):
        arrive(left.at[(y + 4 - step) % 4], a2_r.at[step - 1])

    for c in range(NC):
        ring_close(0, c)
        part1[c] = product(0, c)
        for h in range(2):
            to_x = (2 * core + h + 4 - zi) % 4
            for other in range(2):
                send(
                    part1.at[c, pl.ds(192 * h + 96 * other, 96)], got1.at[c, x],
                    r1_s.at[4 * c + 2 * h + other], r1_r.at[4 * c + x], device(x_=to_x, core_=other),
                    here=jnp.logical_and(to_x == x, core == other),
                )
    for c in range(NC):
        for other in range(4):
            arrive(got1.at[c, other], r1_r.at[4 * c + other])
        total = (got1[c, 0] + got1[c, 1]) + (got1[c, 2] + got1[c, 3])
        rounded = (total * slab_mask[:, BS * c:BS * (c + 1)]).astype(BF16)
        right2[c, pl.ds(own_rows, 96)] = rounded
        square[:, BS * c:BS * (c + 1)] = rounded
        ring_open(1, c)
    for h in range(2):
        send(
            square.at[pl.ds(48 * h, 48)], square_got.at[kind % 2], sq_s.at[h], sq_r.at[kind % 2],
            device(x_=2 * core + h, core_=kind // 2),
            here=jnp.logical_and(2 * core + h == x, kind // 2 == core),
        )
    for hop in range(1, 5):
        for c in range(NC):
            ring_hop(1, c, hop)

    for c in range(NC):
        ring_close(1, c)
        total = product(1, c)
        for h in range(2):
            for k in range(4):
                part2[c, k, h] = total[192 * h + 48 * k:192 * h + 48 * (k + 1)]
        for step in range(1, 4):
            to_x = (x + step) % 4
            send(part2.at[c, to_x], got2.at[c, step - 1], r2_s.at[3 * c + step - 1], r2_r.at[3 * c + step - 1],
                 device(x_=to_x))
    for h in range(2):
        arrive(square_got.at[h], sq_r.at[h])
    for c in range(NC):
        for step in range(1, 4):
            arrive(got2.at[c, step - 1], r2_r.at[3 * c + step - 1])
        for h in range(2):
            total = (part2[c, x, h] + got2[c, 0, h]) + (got2[c, 1, h] + got2[c, 2, h])
            cube = total * out_mask[h, :, BS * c:BS * (c + 1)]
            final[c, h] = 3.0 * square_got[h, :, BS * c:BS * (c + 1)].astype(F32) - 2.0 * cube
            send(
                final.at[c, h], final_got.at[c, zi % 2], f_s.at[2 * c + h], f_r.at[2 * c + zi % 2],
                device(zi_=2 * core + h, core_=zi // 2),
                here=jnp.logical_and(2 * core + h == zi, zi // 2 == core),
            )
    for c in range(NC):
        for e in range(2):
            arrive(final_got.at[c, e], f_r.at[2 * c + e])
            out[:, 384 * e + BS * c:384 * e + BS * (c + 1)] = final_got[c, e]
    for copy, go in pending:
        if go is None:
            copy.wait_send()
        else:
            pl.when(go)(copy.wait_send)


def shards(density, occupancy):
    dma = pltpu.SemaphoreType.DMA
    return pl.pallas_call(
        kernel,
        name="purify",
        out_shape=jax.ShapeDtypeStruct((48, 768), F32),
        in_specs=[pl.BlockSpec(memory_space=pltpu.VMEM)] * 2,
        out_specs=pl.BlockSpec(memory_space=pltpu.VMEM),
        scratch_shapes=[
            pltpu.VMEM((384, 768), BF16),
            pltpu.VMEM((4, 384, 384), BF16),
            pltpu.VMEM((NC, 1536, BS), BF16),
            pltpu.VMEM((NC, 1536, BS), BF16),
            pltpu.VMEM((NC, 384, BS), F32),
            pltpu.VMEM((NC, 4, 96, BS), F32),
            pltpu.VMEM((96, 384), BF16),
            pltpu.VMEM((2, 48, 384), BF16),
            pltpu.VMEM((NC, 4, 2, 48, BS), F32),
            pltpu.VMEM((NC, 3, 2, 48, BS), F32),
            pltpu.VMEM((NC, 2, 48, BS), F32),
            pltpu.VMEM((NC, 2, 48, BS), F32),
            pltpu.VMEM((96, 384), F32),
            pltpu.VMEM((2, 48, 384), F32),
            dma((2,)), dma((2,)), dma((3,)), dma((3,)), dma((2 * NC,)), dma((NC,)),
            dma((16 * NC,)), dma((16 * NC,)), dma((18 * NC,)), dma((18 * NC,)),
            dma((4 * NC,)), dma((4 * NC,)), dma((2,)), dma((2,)),
            dma((3 * NC,)), dma((3 * NC,)), dma((2 * NC,)), dma((2 * NC,)),
        ],
        compiler_params=pltpu.CompilerParams(
            collective_id=0, has_side_effects=True, vmem_limit_bytes=32 * 1024 * 1024
        ),
        cost_estimate=pl.CostEstimate(flops=2 * 2 * 384 * 384 * 1536, bytes_accessed=2 * 384 * 768 + 4 * 48 * 768,
                                      transcendentals=0),
    )(density, occupancy)


def solution(mesh):
    return jax.shard_map(
        shards,
        mesh=mesh,
        in_specs=(P("row", "col"), P()),
        out_specs=P(("row", "layer"), "col"),
        check_vma=False,
    )
```

```python
import jax
import jax.numpy as jnp
from jax import lax
from jax.experimental import pallas as pl
from jax.experimental.pallas import tpu as pltpu
from jax.sharding import PartitionSpec as P

MESH = pl.DeviceIdType.MESH
BS = 128
NC = 3
F32 = jnp.float32
BF16 = jnp.bfloat16


def kernel(density, occupancy, out, tile, left, right1, right2, part1, got1, square, square_got, part2, got2,
           final, final_got, slab_mask, out_mask,
           a1_s, a1_r, a2_s, a2_r, seed_s, seed_r, ring_s, ring_r, sib_s, sib_r,
           r1_s, r1_r, sq_s, sq_r, r2_s, r2_r, f_s, f_r):
    row, col, layer = (lax.axis_index(name) for name in ("row", "col", "layer"))
    group, zi = row // 4, row % 4
    y, core = col // 2, col % 2
    zh, x = layer // 4, layer % 4
    place = 4 * zh + group
    kind = (x + zi) % 4
    rights = (right1, right2)

    def device(x_=x, y_=y, core_=core, place_=place, zi_=zi):
        return {"row": 4 * (place_ % 4) + zi_, "col": 2 * y_ + core_, "layer": 4 * (place_ // 4) + x_}

    sibling = device(core_=1 - core)
    up, down = device(place_=(place + 1) % 8), device(place_=(place + 7) % 8)

    barrier = pltpu.get_barrier_semaphore()
    friends = [sibling, up, down]
    for step in range(1, 4):
        friends.append(device(y_=(y + step) % 4))
        for other in range(2):
            friends.append(device(zi_=(zi + step) % 4, core_=other))
            friends.append(device(x_=(x + step) % 4, core_=other))
    for friend in friends:
        pl.semaphore_signal(barrier, inc=1, device_id=friend, device_id_type=MESH)

    pattern = occupancy[...].astype(F32).astype(BF16)
    blocks = pattern.shape[0]

    def mask(row0, rows, col0, cols):
        row_block = (row0 + lax.broadcasted_iota(jnp.int32, (rows, blocks), 0)) // BS
        rows_hot = (row_block == lax.broadcasted_iota(jnp.int32, (rows, blocks), 1)).astype(F32).astype(BF16)
        col_block = (col0 + lax.broadcasted_iota(jnp.int32, (blocks, cols), 1)) // BS
        cols_hot = (col_block == lax.broadcasted_iota(jnp.int32, (blocks, cols), 0)).astype(F32).astype(BF16)
        chosen = jnp.dot(rows_hot, pattern, preferred_element_type=F32).astype(BF16)
        return jnp.dot(chosen, cols_hot, preferred_element_type=F32)

    tile[...] = density[...] * mask(384 * row, 384, 768 * col, 768).astype(BF16)
    pl.semaphore_wait(barrier, len(friends))

    pending = []

    def send(src, dst, send_sem, recv_sem, target, here=None, only=None):
        copy = pltpu.make_async_remote_copy(
            src_ref=src, dst_ref=dst, send_sem=send_sem, recv_sem=recv_sem, device_id=target, device_id_type=MESH
        )
        if here is None:
            go = only
        else:
            go = jnp.logical_not(here) if only is None else jnp.logical_and(only, jnp.logical_not(here))

            @pl.when(here if only is None else jnp.logical_and(only, here))
            def _():
                pltpu.make_async_copy(src, dst, recv_sem).start()

        if go is None:
            copy.start()
        else:
            pl.when(go)(copy.start)
        pending.append((copy, go))

    def arrive(dst, recv_sem):
        pltpu.make_async_remote_copy(
            src_ref=dst, dst_ref=dst, send_sem=recv_sem, recv_sem=recv_sem, device_id=sibling, device_id_type=MESH
        ).wait_recv()

    seed_zi = (zi + 4 - x) % 4

    def seeds(c):
        for other in range(2):
            send(
                tile.at[pl.ds(192 * other, 192), pl.ds(pl.multiple_of(384 * (seed_zi % 2) + BS * c, BS), BS)],
                right1.at[c, pl.ds(pl.multiple_of(384 * group + 192 * other, 64), 192)],
                seed_s.at[2 * c + other], seed_r.at[c], device(zi_=seed_zi, core_=other),
                here=jnp.logical_and(seed_zi == zi, core == other), only=core == seed_zi // 2,
            )

    def left_group():
        for h in range(2):
            to_zi = (2 * core + h + 4 - x) % 4
            send(
                tile.at[pl.ds(pl.multiple_of(192 * zh, 64), 192), pl.ds(384 * h, 384)],
                left.at[y, pl.ds(pl.multiple_of(192 * (zi % 2), 64), 192)],
                a1_s.at[h], a1_r.at[zi % 2], device(zi_=to_zi, core_=zi // 2),
                here=jnp.logical_and(to_zi == zi, zi // 2 == core),
            )

    def left_open():
        for h in range(2):
            arrive(left.at[y, pl.ds(192 * h, 192)], a1_r.at[h])
        for way in range(2):
            send(left.at[y], left.at[y], a2_s.at[way], a2_r.at[way], device(y_=(y + (3 if way else 1)) % 4))

    def left_hop():
        for way in range(2):
            came = (y + (1 if way else 3)) % 4
            arrive(left.at[came], a2_r.at[way])
            ref = left.at[came, pl.ds(192 * way, 192)]
            send(ref, ref, a2_s.at[2 + way], a2_r.at[2 + way], device(y_=(y + (3 if way else 1)) % 4))

    def left_close():
        for way in range(2):
            arrive(left.at[(y + 2) % 4, pl.ds(192 * way, 192)], a2_r.at[2 + way])

    hops = (2, 4)

    def span(q, way, hop, core_, narrow):
        away = (place + (8 - hop if way == 0 else hop)) % 8
        if q == 0:
            start, size = 384 * (away % 4) + 192 * core_, 192
        else:
            start, size = 384 * (away % 4) + 192 * (away // 4) + 96 * core_, 96
        if narrow:
            size //= 2
            start = start + size * way
        return pl.ds(pl.multiple_of(start, 16), size)

    def ring_number(q, c, way, hop):
        return 4 * NC * q + (2 * c + way) * hops[q] + hop - 1

    def share_number(q, c, way, hop):
        return 5 * NC * q + (2 * hops[q] + 1) * c + (0 if hop == 0 else 1 + way * hops[q] + hop - 1)

    def ring_send(q, c, way, hop):
        ref = rights[q].at[c, span(q, way, hop - 1, core, hop == hops[q])]
        n = ring_number(q, c, way, hop)
        send(ref, ref, ring_s.at[n], ring_r.at[n], down if way else up)

    def share(q, c, way, hop):
        ref = rights[q].at[c, span(q, way, hop, core, hop == hops[q])]
        n = share_number(q, c, way, hop)
        send(ref, ref, sib_s.at[n], sib_r.at[n], sibling)

    def ring_open(q, c):
        ring_send(q, c, 0, 1)
        ring_send(q, c, 1, 1)
        share(q, c, 0, 0)

    def ring_hop(q, c, hop):
        for way in range(2):
            arrive(rights[q].at[c, span(q, way, hop, core, hop == hops[q])], ring_r.at[ring_number(q, c, way, hop)])
            if hop < hops[q]:
                ring_send(q, c, way, hop + 1)
            share(q, c, way, hop)

    def ring_close(q, c):
        for hop in range(hops[q] + 1):
            for way in range(2 if hop else 1):
                arrive(rights[q].at[c, span(q, way, hop, 1 - core, hop == hops[q])], sib_r.at[share_number(q, c, way, hop)])

    def seed_open(c):
        arrive(right1.at[c, span(0, 0, 0, core, False)], seed_r.at[c])
        ring_open(0, c)

    def product(q, c):
        total = jnp.dot(left[0], rights[q][c, pl.ds(0, 384)], preferred_element_type=F32)
        for j in range(1, 4):
            total += jnp.dot(left[j], rights[q][c, pl.ds(384 * j, 384)], preferred_element_type=F32)
        return total

    def masks():
        slab_mask[...] = mask(384 * (4 * group + kind) + 192 * zh + 96 * core, 96, 1536 * y + 384 * zi, 384)
        for h in range(2):
            out_mask[h] = mask(384 * (4 * group + 2 * core + h) + 192 * zh + 48 * x, 48, 1536 * y + 384 * zi, 384)

    def square_part(c):
        ring_close(0, c)
        part1[c] = product(0, c)
        for h in range(2):
            to_x = (2 * core + h + 4 - zi) % 4
            for other in range(2):
                send(
                    part1.at[c, pl.ds(192 * h + 96 * other, 96)], got1.at[c, x],
                    r1_s.at[4 * c + 2 * h + other], r1_r.at[4 * c + x], device(x_=to_x, core_=other),
                    here=jnp.logical_and(to_x == x, core == other),
                )

    def square_sum(c):
        for other in range(4):
            arrive(got1.at[c, other], r1_r.at[4 * c + other])
        total = (got1[c, 0] + got1[c, 1]) + (got1[c, 2] + got1[c, 3])
        rounded = (total * slab_mask[:, BS * c:BS * (c + 1)]).astype(BF16)
        right2[c, span(1, 0, 0, core, False)] = rounded
        square[:, BS * c:BS * (c + 1)] = rounded
        ring_open(1, c)

    def square_rows():
        for h in range(2):
            send(
                square.at[pl.ds(48 * h, 48)], square_got.at[kind % 2], sq_s.at[h], sq_r.at[kind % 2],
                device(x_=2 * core + h, core_=kind // 2),
                here=jnp.logical_and(2 * core + h == x, kind // 2 == core),
            )

    def cube_part(c):
        ring_close(1, c)
        total = product(1, c)
        for h in range(2):
            for k in range(4):
                part2[c, k, h] = total[192 * h + 48 * k:192 * h + 48 * (k + 1)]
        for step in range(1, 4):
            to_x = (x + step) % 4
            send(part2.at[c, to_x], got2.at[c, step - 1], r2_s.at[3 * c + step - 1], r2_r.at[3 * c + step - 1],
                 device(x_=to_x))

    def cube_sum(c):
        for step in range(1, 4):
            arrive(got2.at[c, step - 1], r2_r.at[3 * c + step - 1])
        for h in range(2):
            total = (part2[c, x, h] + got2[c, 0, h]) + (got2[c, 1, h] + got2[c, 2, h])
            cube = total * out_mask[h, :, BS * c:BS * (c + 1)]
            final[c, h] = 3.0 * square_got[h, :, BS * c:BS * (c + 1)].astype(F32) - 2.0 * cube
            send(
                final.at[c, h], final_got.at[c, zi % 2], f_s.at[2 * c + h], f_r.at[2 * c + zi % 2],
                device(zi_=2 * core + h, core_=zi // 2),
                here=jnp.logical_and(2 * core + h == zi, zi // 2 == core),
            )

    def finish(c):
        for e in range(2):
            arrive(final_got.at[c, e], f_r.at[2 * c + e])
            out[:, 384 * e + BS * c:384 * e + BS * (c + 1)] = final_got[c, e]

    seeds(0)
    left_group()
    seeds(1)
    seeds(2)
    seed_open(0)
    left_open()
    seed_open(1)
    masks()
    ring_hop(0, 0, 1)
    seed_open(2)
    left_hop()
    ring_hop(0, 0, 2)
    ring_hop(0, 1, 1)
    left_close()
    square_part(0)
    ring_hop(0, 1, 2)
    ring_hop(0, 2, 1)
    square_part(1)
    square_sum(0)
    ring_hop(0, 2, 2)
    square_part(2)
    square_sum(1)
    ring_hop(1, 0, 1)
    square_sum(2)
    square_rows()
    ring_hop(1, 1, 1)
    ring_hop(1, 0, 2)
    ring_hop(1, 2, 1)
    ring_hop(1, 1, 2)
    ring_hop(1, 0, 3)
    ring_hop(1, 2, 2)
    ring_hop(1, 1, 3)
    ring_hop(1, 0, 4)
    ring_hop(1, 2, 3)
    ring_hop(1, 1, 4)
    cube_part(0)
    ring_hop(1, 2, 4)
    cube_part(1)
    for h in range(2):
        arrive(square_got.at[h], sq_r.at[h])
    cube_part(2)
    cube_sum(0)
    cube_sum(1)
    cube_sum(2)
    for c in range(NC):
        finish(c)
    for copy, go in pending:
        if go is None:
            copy.wait_send()
        else:
            pl.when(go)(copy.wait_send)


def shards(density, occupancy):
    dma = pltpu.SemaphoreType.DMA
    return pl.pallas_call(
        kernel,
        name="purify",
        out_shape=jax.ShapeDtypeStruct((48, 768), F32),
        in_specs=[pl.BlockSpec(memory_space=pltpu.VMEM)] * 2,
        out_specs=pl.BlockSpec(memory_space=pltpu.VMEM),
        scratch_shapes=[
            pltpu.VMEM((384, 768), BF16),
            pltpu.VMEM((4, 384, 384), BF16),
            pltpu.VMEM((NC, 1536, BS), BF16),
            pltpu.VMEM((NC, 1536, BS), BF16),
            pltpu.VMEM((NC, 384, BS), F32),
            pltpu.VMEM((NC, 4, 96, BS), F32),
            pltpu.VMEM((96, 384), BF16),
            pltpu.VMEM((2, 48, 384), BF16),
            pltpu.VMEM((NC, 4, 2, 48, BS), F32),
            pltpu.VMEM((NC, 3, 2, 48, BS), F32),
            pltpu.VMEM((NC, 2, 48, BS), F32),
            pltpu.VMEM((NC, 2, 48, BS), F32),
            pltpu.VMEM((96, 384), F32),
            pltpu.VMEM((2, 48, 384), F32),
            dma((2,)), dma((2,)), dma((4,)), dma((4,)), dma((2 * NC,)), dma((NC,)),
            dma((12 * NC,)), dma((12 * NC,)), dma((14 * NC,)), dma((14 * NC,)),
            dma((4 * NC,)), dma((4 * NC,)), dma((2,)), dma((2,)),
            dma((3 * NC,)), dma((3 * NC,)), dma((2 * NC,)), dma((2 * NC,)),
        ],
        compiler_params=pltpu.CompilerParams(
            collective_id=0, has_side_effects=True, vmem_limit_bytes=32 * 1024 * 1024
        ),
        cost_estimate=pl.CostEstimate(flops=2 * 2 * 384 * 384 * 1536, bytes_accessed=2 * 384 * 768 + 4 * 48 * 768,
                                      transcendentals=0),
    )(density, occupancy)


def solution(mesh):
    return jax.shard_map(
        shards,
        mesh=mesh,
        in_specs=(P("row", "col"), P()),
        out_specs=P(("row", "layer"), "col"),
        check_vma=False,
    )
```

```python
import jax
import jax.numpy as jnp
from jax import lax
from jax.experimental import pallas as pl
from jax.experimental.pallas import tpu as pltpu
from jax.sharding import PartitionSpec as P

MESH = pl.DeviceIdType.MESH
BS = 128
NC = 3
NP = 4
ROWS = 384 // NP
F32 = jnp.float32
BF16 = jnp.bfloat16


def kernel(density, occupancy, out, tile, left, right1, right2, part1, got1, square, part2, got2, final, final_got,
           slab_mask, a1_s, a1_r, a2_s, a2_r, a3_s, a3_r, seed_s, seed_r, ring_s, ring_r,
           r1_s, r1_r, sq_s, sq_r, r2_s, r2_r, f_s, f_r):
    row, col, layer = (lax.axis_index(name) for name in ("row", "col", "layer"))
    y, core = col // 2, col % 2
    zh, x = layer // 4, layer % 4
    z = 16 * zh + row
    pair, zi = z // 2, z % 2
    low = pair % 8
    kind = (x + zi) % 4
    is_root = kind // 2 == pair % 2
    not_root = jnp.logical_not(is_root)
    rights = (right1, right2)

    def device(x_=x, y_=y, core_=core, z_=z):
        return {"row": z_ % 16, "col": 2 * y_ + core_, "layer": 4 * (z_ // 16) + x_}

    def mate(zi_, core_):
        return device(z_=2 * pair + zi_, core_=core_)

    sibling = device(core_=1 - core)
    ahead = (device(z_=(z + 2) % 32), device(z_=(z + 30) % 32))
    beside = (device(y_=(y + 1) % 4), device(y_=(y + 3) % 4))

    barrier = pltpu.get_barrier_semaphore()
    friends = [sibling, mate(1 - zi, 0), mate(1 - zi, 1), *ahead, *beside]
    friends += [device(x_=(x + step) % 4) for step in range(1, 4)]
    for friend in friends:
        pl.semaphore_signal(barrier, inc=1, device_id=friend, device_id_type=MESH)

    pattern = occupancy[...].astype(F32).astype(BF16)
    blocks = pattern.shape[0]

    def mask(row0, rows, col0, cols):
        row_block = (row0 + lax.broadcasted_iota(jnp.int32, (rows, blocks), 0)) // BS
        rows_hot = (row_block == lax.broadcasted_iota(jnp.int32, (rows, blocks), 1)).astype(F32).astype(BF16)
        col_block = (col0 + lax.broadcasted_iota(jnp.int32, (blocks, cols), 1)) // BS
        cols_hot = (col_block == lax.broadcasted_iota(jnp.int32, (blocks, cols), 0)).astype(F32).astype(BF16)
        chosen = jnp.dot(rows_hot, pattern, preferred_element_type=F32).astype(BF16)
        return jnp.dot(chosen, cols_hot, preferred_element_type=F32)

    tile[...] = density[...] * mask(384 * row, 384, 768 * col, 768).astype(BF16)
    pl.semaphore_wait(barrier, len(friends))

    pending = []

    def send(src, dst, send_sem, recv_sem, target, here=None, only=None):
        copy = pltpu.make_async_remote_copy(
            src_ref=src, dst_ref=dst, send_sem=send_sem, recv_sem=recv_sem, device_id=target, device_id_type=MESH
        )
        if here is None:
            go = only
        else:
            go = jnp.logical_not(here) if only is None else jnp.logical_and(only, jnp.logical_not(here))

            @pl.when(here if only is None else jnp.logical_and(only, here))
            def _():
                pltpu.make_async_copy(src, dst, recv_sem).start()

        if go is None:
            copy.start()
        else:
            pl.when(go)(copy.start)
        pending.append((copy, go))

    def arrive(dst, recv_sem):
        pltpu.make_async_remote_copy(
            src_ref=dst, dst_ref=dst, send_sem=recv_sem, recv_sem=recv_sem, device_id=sibling, device_id_type=MESH
        ).wait_recv()

    seed_zi = (row + 4 - x % 4) % 4

    def seeds(c):
        for other in range(2):
            send(
                tile.at[:, pl.ds(384 * other + BS * c, BS)],
                right1.at[c, pl.ds(pl.multiple_of(384 * (low // 2), 128), 384)],
                seed_s.at[2 * c + other], seed_r.at[c], mate(seed_zi % 2, other),
                here=jnp.logical_and(seed_zi == zi, core == other),
                only=jnp.logical_and(seed_zi < 2, core == seed_zi),
            )

    def left_rows(j, core_, start=0, size=384):
        return left.at[j, pl.ds(pl.multiple_of(384 * core_ + start, 64), size)]

    def left_group():
        for to_zi in range(2):
            to_kind = (x + to_zi) % 4
            send(
                tile.at[:, pl.ds(pl.multiple_of(384 * (to_kind % 2), BS), 384)], left_rows(y, zi),
                a1_s.at[to_zi], a1_r.at[0], mate(to_zi, zi),
                here=jnp.logical_and(zi == to_zi, core == zi), only=core == to_kind // 2,
            )

    def left_share(j, n, start=0, size=384):
        ref = left_rows(j, core, start, size)
        send(ref, ref, a3_s.at[n], a3_r.at[n], sibling)

    def left_open():
        ref = left_rows(y, core)
        arrive(ref, a1_r.at[0])
        for way in range(2):
            send(ref, ref, a2_s.at[way], a2_r.at[way], beside[way])
        left_share(y, 0)

    def left_hop():
        for way in range(2):
            came = (y + (1 if way else 3)) % 4
            arrive(left_rows(came, core), a2_r.at[way])
            ref = left_rows(came, core, 192 * way, 192)
            send(ref, ref, a2_s.at[2 + way], a2_r.at[2 + way], beside[way])
            left_share(came, 1 + way)

    def left_last():
        for way in range(2):
            arrive(left_rows((y + 2) % 4, core, 192 * way, 192), a2_r.at[2 + way])
            left_share((y + 2) % 4, 3 + way, 192 * way, 192)

    def left_close():
        arrive(left_rows(y, 1 - core), a3_r.at[0])
        for way in range(2):
            arrive(left_rows((y + (1 if way else 3)) % 4, 1 - core), a3_r.at[1 + way])
            arrive(left_rows((y + 2) % 4, 1 - core, 192 * way, 192), a3_r.at[3 + way])

    def ring_rows(way, stage, piece):
        far = jnp.where(is_root, 2 * stage, 2 * stage - 1)
        from_pair = (pair + (far if way else 16 - far)) % 16
        return pl.ds(pl.multiple_of(384 * ((from_pair % 8) // 2) + ROWS * piece, 32), ROWS)

    def ring_number(q, c, way, stage, piece):
        return (((q * NC + c) * 2 + way) * 2 + stage - 1) * NP + piece

    def is_half(way, piece):
        return piece * 2 // NP == way

    def own_rows(piece=0, size=384):
        return pl.ds(pl.multiple_of(384 * (low // 2) + ROWS * piece, 32), size)

    def ring_open(q, c):
        for piece in range(NP):
            for way in range(2):
                ref = rights[q].at[c, own_rows(piece, ROWS)]
                send(ref, ref, ring_s.at[(((q * NC + c) * 2 + way) * 3) * NP + piece],
                     ring_r.at[ring_number(q, c, way, 1, piece)], ahead[way], only=is_root)

    def ring_first(q, c):
        for piece in range(NP):
            for way in range(2):
                n = ring_number(q, c, way, 1, piece)
                ref = rights[q].at[c, ring_rows(way, 1, piece)]
                arrive(ref, ring_r.at[n])
                send(ref, ref, ring_s.at[(((q * NC + c) * 2 + way) * 3 + 1) * NP + piece],
                     ring_r.at[n + jnp.where(is_root, NP, 0)], ahead[way])

    def ring_second(q, c):
        for piece in range(NP):
            for way in range(2):
                n = ring_number(q, c, way, 2, piece)
                ref = rights[q].at[c, ring_rows(way, 2, piece)]
                if is_half(way, piece):
                    arrive(ref, ring_r.at[n])
                    send(ref, ref, ring_s.at[(((q * NC + c) * 2 + way) * 3 + 2) * NP + piece], ring_r.at[n],
                         ahead[way], only=not_root)
                else:
                    pl.when(not_root)(lambda ref=ref, n=n: arrive(ref, ring_r.at[n]))

    def seed_open(c):
        pl.when(is_root)(lambda: arrive(right1.at[c, own_rows()], seed_r.at[c]))
        ring_open(0, c)

    def masks():
        for a in range(2):
            for h in range(2):
                slab_mask[a, h] = mask(384 * (2 * low + a) + 192 * h + 48 * x, 48, 1536 * y + 768 * zi + 384 * core, 384)

    def square_part(c):
        total = jnp.dot(left[0], right1[c, pl.ds(0, 384)], preferred_element_type=F32)
        for j in range(1, 4):
            total += jnp.dot(left[j], right1[c, pl.ds(384 * j, 384)], preferred_element_type=F32)
        for a in range(2):
            for h in range(2):
                for k in range(4):
                    part1[c, k, a, h] = total[384 * a + 192 * h + 48 * k:384 * a + 192 * h + 48 * (k + 1)]
        for step in range(1, 4):
            to_x = (x + step) % 4
            send(part1.at[c, to_x], got1.at[c, step - 1], r1_s.at[3 * c + step - 1], r1_r.at[3 * c + step - 1],
                 device(x_=to_x))

    def square_sum(c):
        for step in range(1, 4):
            arrive(got1.at[c, step - 1], r1_r.at[3 * c + step - 1])
        for a in range(2):
            to_x = (2 * low + a + 4 - zi) % 4
            for h in range(2):
                total = (part1[c, x, a, h] + got1[c, 0, a, h]) + (got1[c, 1, a, h] + got1[c, 2, a, h])
                square[c, a, h] = (total * slab_mask[a, h, :, BS * c:BS * (c + 1)]).astype(BF16)
                send(
                    square.at[c, a, h],
                    right2.at[c, pl.ds(pl.multiple_of(384 * (low // 2) + 192 * h + 48 * x, 16), 48)],
                    sq_s.at[4 * c + 2 * a + h], sq_r.at[8 * c + 2 * x + h], device(x_=to_x), here=to_x == x,
                )

    def square_open(c):
        def slabs():
            for k in range(4):
                for h in range(2):
                    arrive(right2.at[c, pl.ds(pl.multiple_of(384 * (low // 2) + 192 * h + 48 * k, 16), 48)],
                           sq_r.at[8 * c + 2 * k + h])

        pl.when(is_root)(slabs)
        ring_open(1, c)

    def cube_part(c):
        for a in range(2):
            rows = pl.ds(pl.multiple_of(384 * a + 192 * zh, 64), 192)
            total = jnp.dot(left[0, rows], right2[c, pl.ds(0, 384)], preferred_element_type=F32)
            for j in range(1, 4):
                total += jnp.dot(left[j, rows], right2[c, pl.ds(384 * j, 384)], preferred_element_type=F32)
            for k in range(4):
                part2[c, k, a] = total[48 * k:48 * (k + 1)]
        for step in range(1, 4):
            to_x = (x + step) % 4
            send(part2.at[c, to_x], got2.at[c, step - 1], r2_s.at[3 * c + step - 1], r2_r.at[3 * c + step - 1],
                 device(x_=to_x))

    def cube_sum(c):
        for step in range(1, 4):
            arrive(got2.at[c, step - 1], r2_r.at[3 * c + step - 1])
        for a in range(2):
            total = (part2[c, x, a] + got2[c, 0, a]) + (got2[c, 1, a] + got2[c, 2, a])
            cube = total * slab_mask[a, zh, :, BS * c:BS * (c + 1)]
            final[c, a] = 3.0 * square[c, a, zh].astype(F32) - 2.0 * cube
            send(
                final.at[c, a], final_got.at[c, core], f_s.at[2 * c + a], f_r.at[2 * c + core], mate(a, zi),
                here=jnp.logical_and(zi == a, core == zi),
            )

    def finish(c):
        for e in range(2):
            arrive(final_got.at[c, e], f_r.at[2 * c + e])
            out[:, 384 * e + BS * c:384 * e + BS * (c + 1)] = final_got[c, e]

    seeds(0)
    left_group()
    seeds(1)
    seeds(2)
    seed_open(0)
    left_open()
    seed_open(1)
    ring_first(0, 0)
    seed_open(2)
    masks()
    left_hop()
    ring_first(0, 1)
    ring_second(0, 0)
    left_last()
    left_close()
    square_part(0)
    ring_first(0, 2)
    ring_second(0, 1)
    square_part(1)
    square_sum(0)
    ring_second(0, 2)
    square_part(2)
    square_sum(1)
    square_open(0)
    square_sum(2)
    square_open(1)
    ring_first(1, 0)
    square_open(2)
    ring_first(1, 1)
    ring_second(1, 0)
    cube_part(0)
    ring_first(1, 2)
    ring_second(1, 1)
    cube_part(1)
    cube_sum(0)
    ring_second(1, 2)
    cube_part(2)
    cube_sum(1)
    cube_sum(2)
    for c in range(NC):
        finish(c)
    for copy, go in pending:
        if go is None:
            copy.wait_send()
        else:
            pl.when(go)(copy.wait_send)


def shards(density, occupancy):
    dma = pltpu.SemaphoreType.DMA
    return pl.pallas_call(
        kernel,
        name="purify",
        out_shape=jax.ShapeDtypeStruct((48, 768), F32),
        in_specs=[pl.BlockSpec(memory_space=pltpu.VMEM)] * 2,
        out_specs=pl.BlockSpec(memory_space=pltpu.VMEM),
        scratch_shapes=[
            pltpu.VMEM((384, 768), BF16),
            pltpu.VMEM((4, 768, 384), BF16),
            pltpu.VMEM((NC, 1536, BS), BF16),
            pltpu.VMEM((NC, 1536, BS), BF16),
            pltpu.VMEM((NC, 4, 2, 2, 48, BS), F32),
            pltpu.VMEM((NC, 3, 2, 2, 48, BS), F32),
            pltpu.VMEM((NC, 2, 2, 48, BS), BF16),
            pltpu.VMEM((NC, 4, 2, 48, BS), F32),
            pltpu.VMEM((NC, 3, 2, 48, BS), F32),
            pltpu.VMEM((NC, 2, 48, BS), F32),
            pltpu.VMEM((NC, 2, 48, BS), F32),
            pltpu.VMEM((2, 2, 48, 384), F32),
            dma((2,)), dma((1,)), dma((4,)), dma((4,)), dma((5,)), dma((5,)), dma((2 * NC,)), dma((NC,)),
            dma((12 * NC * NP,)), dma((8 * NC * NP,)),
            dma((3 * NC,)), dma((3 * NC,)), dma((4 * NC,)), dma((8 * NC,)),
            dma((3 * NC,)), dma((3 * NC,)), dma((2 * NC,)), dma((2 * NC,)),
        ],
        compiler_params=pltpu.CompilerParams(
            collective_id=0, has_side_effects=True, vmem_limit_bytes=32 * 1024 * 1024
        ),
        cost_estimate=pl.CostEstimate(flops=3 * 2 * 384 * 384 * 1536, bytes_accessed=2 * 384 * 768 + 4 * 48 * 768,
                                      transcendentals=0),
    )(density, occupancy)


def solution(mesh):
    return jax.shard_map(
        shards,
        mesh=mesh,
        in_specs=(P("row", "col"), P()),
        out_specs=P(("row", "layer"), "col"),
        check_vma=False,
    )
```

```python
import jax
import jax.numpy as jnp
from jax import lax
from jax.experimental import pallas as pl
from jax.experimental.pallas import tpu as pltpu
from jax.sharding import PartitionSpec as P

MESH = pl.DeviceIdType.MESH
BS = 128
NC = 3
F32 = jnp.float32
BF16 = jnp.bfloat16


def kernel(density, occupancy, out, raw, raw_sem, tile, left, right1, right2, part1, got1, square, square_got, part2, got2,
           final, final_got, slab_mask, out_mask,
           a1_s, a1_r, a2_s, a2_r, seed_s, seed_r, ring_s, ring_r, sib_s, sib_r,
           r1_s, r1_r, sq_s, sq_r, r2_s, r2_r, f_s, f_r):
    row, col, layer = (lax.axis_index(name) for name in ("row", "col", "layer"))
    group, zi = row // 4, row % 4
    y, core = col // 2, col % 2
    zh, x = layer // 4, layer % 4
    place = 4 * zh + group
    kind = (x + zi) % 4
    rights = (right1, right2)

    def device(x_=x, y_=y, core_=core, place_=place, zi_=zi):
        return {"row": 4 * (place_ % 4) + zi_, "col": 2 * y_ + core_, "layer": 4 * (place_ // 4) + x_}

    twist = jnp.where(zi % 2 == 1, 2, -2)
    away = jnp.where(x == 0, 0, jnp.where(x == 1, -1, jnp.where(x == 2, twist, 1)))
    seed_to, seed_from = 4 * place + zi + away + 32, 4 * place + zi - away + 32
    lag = seed_from // 4 - place

    def chip(z_, core_):
        return device(core_=core_, place_=(z_ // 4) % 8, zi_=z_ % 4)

    sibling = device(core_=1 - core)
    up, down = device(place_=(place + 1) % 8), device(place_=(place + 7) % 8)

    load = pltpu.make_async_copy(density, raw, raw_sem.at[0])
    load.start()
    barrier = pltpu.get_barrier_semaphore()
    friends = [sibling, up, down]
    for step in range(1, 4):
        friends.append(device(y_=(y + step) % 4))
        for other in range(2):
            friends.append(device(zi_=(zi + step) % 4, core_=other))
            friends.append(device(x_=(x + step) % 4, core_=other))
    for friend in friends:
        pl.semaphore_signal(barrier, inc=1, device_id=friend, device_id_type=MESH)

    @pl.when(x != 0)
    def _():
        for other in range(2):
            pl.semaphore_signal(barrier, inc=1, device_id=chip(seed_to, other), device_id_type=MESH)
            pl.semaphore_signal(barrier, inc=1, device_id=chip(seed_from, other), device_id_type=MESH)

    pattern = occupancy[...].astype(F32).astype(BF16)
    blocks = pattern.shape[0]

    def mask(row0, rows, col0, cols):
        row_block = (row0 + lax.broadcasted_iota(jnp.int32, (rows, blocks), 0)) // BS
        rows_hot = (row_block == lax.broadcasted_iota(jnp.int32, (rows, blocks), 1)).astype(F32).astype(BF16)
        col_block = (col0 + lax.broadcasted_iota(jnp.int32, (blocks, cols), 1)) // BS
        cols_hot = (col_block == lax.broadcasted_iota(jnp.int32, (blocks, cols), 0)).astype(F32).astype(BF16)
        chosen = jnp.dot(rows_hot, pattern, preferred_element_type=F32).astype(BF16)
        return jnp.dot(chosen, cols_hot, preferred_element_type=F32)

    occupied = mask(384 * row, 384, 768 * col, 768).astype(BF16)
    load.wait()
    tile[...] = raw[...] * occupied
    pl.semaphore_wait(barrier, len(friends) + jnp.where(x == 0, 0, 4))

    pending = []

    def send(src, dst, send_sem, recv_sem, target, here=None, only=None):
        copy = pltpu.make_async_remote_copy(
            src_ref=src, dst_ref=dst, send_sem=send_sem, recv_sem=recv_sem, device_id=target, device_id_type=MESH
        )
        if here is None:
            go = only
        else:
            go = jnp.logical_not(here) if only is None else jnp.logical_and(only, jnp.logical_not(here))

            @pl.when(here if only is None else jnp.logical_and(only, here))
            def _():
                pltpu.make_async_copy(src, dst, recv_sem).start()

        if go is None:
            copy.start()
        else:
            pl.when(go)(copy.start)
        pending.append((copy, go))

    def arrive(dst, recv_sem):
        pltpu.make_async_remote_copy(
            src_ref=dst, dst_ref=dst, send_sem=recv_sem, recv_sem=recv_sem, device_id=sibling, device_id_type=MESH
        ).wait_recv()

    seed_zi = seed_to % 4

    def seeds(c):
        for other in range(2):
            send(
                tile.at[pl.ds(192 * other, 192), pl.ds(pl.multiple_of(384 * (seed_zi % 2) + BS * c, BS), BS)],
                right1.at[c, pl.ds(pl.multiple_of(384 * group + 192 * other, 64), 192)],
                seed_s.at[2 * c + other], seed_r.at[c], chip(seed_to, other),
                here=jnp.logical_and(x == 0, core == other), only=core == seed_zi // 2,
            )

    def left_group():
        for h in range(2):
            to_zi = (2 * core + h + 4 - x) % 4
            send(
                tile.at[pl.ds(pl.multiple_of(192 * zh, 64), 192), pl.ds(384 * h, 384)],
                left.at[y, pl.ds(pl.multiple_of(192 * (zi % 2), 64), 192)],
                a1_s.at[h], a1_r.at[zi % 2], device(zi_=to_zi, core_=zi // 2),
                here=jnp.logical_and(to_zi == zi, zi // 2 == core),
            )

    def left_open():
        for h in range(2):
            arrive(left.at[y, pl.ds(192 * h, 192)], a1_r.at[h])
        for way in range(2):
            send(left.at[y], left.at[y], a2_s.at[way], a2_r.at[way], device(y_=(y + (3 if way else 1)) % 4))

    def left_hop():
        for way in range(2):
            came = (y + (1 if way else 3)) % 4
            arrive(left.at[came], a2_r.at[way])
            ref = left.at[came, pl.ds(192 * way, 192)]
            send(ref, ref, a2_s.at[2 + way], a2_r.at[2 + way], device(y_=(y + (3 if way else 1)) % 4))

    def left_close():
        for way in range(2):
            arrive(left.at[(y + 2) % 4, pl.ds(192 * way, 192)], a2_r.at[2 + way])

    hops = (2, 4)

    def span(q, way, hop, core_, narrow):
        at = (place + (8 - hop if way == 0 else hop)) % 8
        if q == 0:
            start, size = 384 * ((at + lag) % 4) + 192 * core_, 192
        else:
            start, size = 384 * (at % 4) + 192 * (at // 4) + 96 * core_, 96
        if narrow:
            size //= 2
            start = start + size * way
        return pl.ds(pl.multiple_of(start, 16), size)

    def ring_number(q, c, way, hop):
        return 4 * NC * q + (2 * c + way) * hops[q] + hop - 1

    def share_number(q, c, way, hop):
        return 5 * NC * q + (2 * hops[q] + 1) * c + (0 if hop == 0 else 1 + way * hops[q] + hop - 1)

    def ring_send(q, c, way, hop):
        ref = rights[q].at[c, span(q, way, hop - 1, core, hop == hops[q])]
        n = ring_number(q, c, way, hop)
        send(ref, ref, ring_s.at[n], ring_r.at[n], down if way else up)

    def share(q, c, way, hop):
        ref = rights[q].at[c, span(q, way, hop, core, hop == hops[q])]
        n = share_number(q, c, way, hop)
        send(ref, ref, sib_s.at[n], sib_r.at[n], sibling)

    def ring_open(q, c):
        ring_send(q, c, 0, 1)
        ring_send(q, c, 1, 1)
        share(q, c, 0, 0)

    def ring_hop(q, c, hop):
        for way in range(2):
            arrive(rights[q].at[c, span(q, way, hop, core, hop == hops[q])], ring_r.at[ring_number(q, c, way, hop)])
            if hop < hops[q]:
                ring_send(q, c, way, hop + 1)
            share(q, c, way, hop)

    def ring_close(q, c):
        for hop in range(hops[q] + 1):
            for way in range(2 if hop else 1):
                arrive(rights[q].at[c, span(q, way, hop, 1 - core, hop == hops[q])], sib_r.at[share_number(q, c, way, hop)])

    def seed_open(c):
        arrive(right1.at[c, span(0, 0, 0, core, False)], seed_r.at[c])
        ring_open(0, c)

    def product(q, c):
        total = jnp.dot(left[0], rights[q][c, pl.ds(0, 384)], preferred_element_type=F32)
        for j in range(1, 4):
            total += jnp.dot(left[j], rights[q][c, pl.ds(384 * j, 384)], preferred_element_type=F32)
        return total

    def masks():
        slab_mask[...] = mask(384 * (4 * group + kind) + 192 * zh + 96 * core, 96, 1536 * y + 384 * zi, 384)
        for h in range(2):
            out_mask[h] = mask(384 * (4 * group + 2 * core + h) + 192 * zh + 48 * x, 48, 1536 * y + 384 * zi, 384)

    def square_part(c):
        part1[c] = product(0, c)
        for h in range(2):
            to_x = (2 * core + h + 4 - zi) % 4
            for other in range(2):
                send(
                    part1.at[c, pl.ds(192 * h + 96 * other, 96)], got1.at[c, x],
                    r1_s.at[4 * c + 2 * h + other], r1_r.at[4 * c + x], device(x_=to_x, core_=other),
                    here=jnp.logical_and(to_x == x, core == other),
                )

    def square_sum(c):
        for other in range(4):
            arrive(got1.at[c, other], r1_r.at[4 * c + other])
        total = (got1[c, 0] + got1[c, 1]) + (got1[c, 2] + got1[c, 3])
        rounded = (total * slab_mask[:, BS * c:BS * (c + 1)]).astype(BF16)
        right2[c, span(1, 0, 0, core, False)] = rounded
        square[:, BS * c:BS * (c + 1)] = rounded

    def square_rows():
        for h in range(2):
            send(
                square.at[pl.ds(48 * h, 48)], square_got.at[kind % 2], sq_s.at[h], sq_r.at[kind % 2],
                device(x_=2 * core + h, core_=kind // 2),
                here=jnp.logical_and(2 * core + h == x, kind // 2 == core),
            )

    def cube_part(c):
        total = product(1, c)
        for h in range(2):
            for k in range(4):
                part2[c, k, h] = total[192 * h + 48 * k:192 * h + 48 * (k + 1)]
        for step in range(1, 4):
            to_x = (x + step) % 4
            send(part2.at[c, to_x], got2.at[c, step - 1], r2_s.at[3 * c + step - 1], r2_r.at[3 * c + step - 1],
                 device(x_=to_x))

    def cube_sum(c):
        for step in range(1, 4):
            arrive(got2.at[c, step - 1], r2_r.at[3 * c + step - 1])
        for h in range(2):
            total = (part2[c, x, h] + got2[c, 0, h]) + (got2[c, 1, h] + got2[c, 2, h])
            cube = total * out_mask[h, :, BS * c:BS * (c + 1)]
            final[c, h] = 3.0 * square_got[h, :, BS * c:BS * (c + 1)].astype(F32) - 2.0 * cube
            send(
                final.at[c, h], final_got.at[c, zi % 2], f_s.at[2 * c + h], f_r.at[2 * c + zi % 2],
                device(zi_=2 * core + h, core_=zi // 2),
                here=jnp.logical_and(2 * core + h == zi, zi // 2 == core),
            )

    def finish(c):
        for e in range(2):
            arrive(final_got.at[c, e], f_r.at[2 * c + e])
            out[:, 384 * e + BS * c:384 * e + BS * (c + 1)] = final_got[c, e]

    left_group()
    seeds(0)
    seeds(1)
    seed_open(0)
    left_open()
    masks()
    seed_open(1)
    ring_hop(0, 0, 1)
    seeds(2)
    left_hop()
    seed_open(2)
    ring_hop(0, 0, 2)
    ring_hop(0, 1, 1)
    left_close()
    ring_close(0, 0)
    square_part(0)
    ring_hop(0, 2, 1)
    ring_hop(0, 1, 2)
    square_sum(0)
    ring_close(0, 1)
    ring_open(1, 0)
    square_part(1)
    ring_hop(0, 2, 2)
    ring_close(0, 2)
    square_part(2)
    ring_hop(1, 0, 1)
    square_sum(1)
    ring_open(1, 1)
    square_sum(2)
    ring_open(1, 2)
    square_rows()
    ring_hop(1, 0, 2)
    ring_hop(1, 1, 1)
    ring_hop(1, 2, 1)
    ring_hop(1, 0, 3)
    ring_hop(1, 1, 2)
    ring_hop(1, 2, 2)
    ring_hop(1, 1, 3)
    ring_hop(1, 2, 3)
    ring_hop(1, 0, 4)
    ring_close(1, 0)
    cube_part(0)
    ring_hop(1, 1, 4)
    ring_close(1, 1)
    ring_hop(1, 2, 4)
    cube_part(1)
    ring_close(1, 2)
    cube_part(2)
    for h in range(2):
        arrive(square_got.at[h], sq_r.at[h])
    cube_sum(0)
    cube_sum(1)
    cube_sum(2)
    finish(1)
    finish(0)
    finish(2)
    for copy, go in pending:
        if go is None:
            copy.wait_send()
        else:
            pl.when(go)(copy.wait_send)


def shards(density, occupancy):
    dma = pltpu.SemaphoreType.DMA
    return pl.pallas_call(
        kernel,
        name="purify",
        out_shape=jax.ShapeDtypeStruct((48, 768), F32),
        in_specs=[pl.BlockSpec(memory_space=pltpu.HBM), pl.BlockSpec(memory_space=pltpu.VMEM)],
        out_specs=pl.BlockSpec(memory_space=pltpu.VMEM),
        scratch_shapes=[
            pltpu.VMEM((384, 768), BF16),
            dma((1,)),
            pltpu.VMEM((384, 768), BF16),
            pltpu.VMEM((4, 384, 384), BF16),
            pltpu.VMEM((NC, 1536, BS), BF16),
            pltpu.VMEM((NC, 1536, BS), BF16),
            pltpu.VMEM((NC, 384, BS), F32),
            pltpu.VMEM((NC, 4, 96, BS), F32),
            pltpu.VMEM((96, 384), BF16),
            pltpu.VMEM((2, 48, 384), BF16),
            pltpu.VMEM((NC, 4, 2, 48, BS), F32),
            pltpu.VMEM((NC, 3, 2, 48, BS), F32),
            pltpu.VMEM((NC, 2, 48, BS), F32),
            pltpu.VMEM((NC, 2, 48, BS), F32),
            pltpu.VMEM((96, 384), F32),
            pltpu.VMEM((2, 48, 384), F32),
            dma((2,)), dma((2,)), dma((4,)), dma((4,)), dma((2 * NC,)), dma((NC,)),
            dma((12 * NC,)), dma((12 * NC,)), dma((14 * NC,)), dma((14 * NC,)),
            dma((4 * NC,)), dma((4 * NC,)), dma((2,)), dma((2,)),
            dma((3 * NC,)), dma((3 * NC,)), dma((2 * NC,)), dma((2 * NC,)),
        ],
        compiler_params=pltpu.CompilerParams(
            collective_id=0, has_side_effects=True, vmem_limit_bytes=60 * 1024 * 1024
        ),
        cost_estimate=pl.CostEstimate(flops=2 * 2 * 384 * 384 * 1536, bytes_accessed=2 * 384 * 768 + 4 * 48 * 768,
                                      transcendentals=0),
    )(density, occupancy)


def solution(mesh):
    return jax.shard_map(
        shards,
        mesh=mesh,
        in_specs=(P("row", "col"), P()),
        out_specs=P(("row", "layer"), "col"),
        check_vma=False,
    )
```

```python
import jax
import jax.numpy as jnp
from jax import lax
from jax.experimental import pallas as pl
from jax.experimental.pallas import tpu as pltpu
from jax.sharding import PartitionSpec as P

MESH = pl.DeviceIdType.MESH
BS = 128
NC = 3
F32 = jnp.float32
BF16 = jnp.bfloat16


def kernel(density, occupancy, out, raw, raw_sem, tile, left, right1, right2, part1, got1, square, square_got, part2, got2,
           final, final_got, slab_mask, out_mask, early,
           a1_s, a1_r, a2_s, a2_r, seed_s, seed_r, ring_s, ring_r, sib_s, sib_r,
           r1_s, r1_r, sq_s, sq_r, r2_s, r2_r, f_s, f_r):
    row, col, layer = (lax.axis_index(name) for name in ("row", "col", "layer"))
    group, zi = row // 4, row % 4
    y, core = col // 2, col % 2
    zh, x = layer // 4, layer % 4
    place = 4 * zh + group
    kind = (x + zi) % 4
    rights = (right1, right2)

    def device(x_=x, y_=y, core_=core, place_=place, zi_=zi):
        return {"row": 4 * (place_ % 4) + zi_, "col": 2 * y_ + core_, "layer": 4 * (place_ // 4) + x_}

    twist = jnp.where(zi % 2 == 1, 2, -2)
    away = jnp.where(x == 0, 0, jnp.where(x == 1, -1, jnp.where(x == 2, twist, 1)))
    seed_to, seed_from = 4 * place + zi + away + 32, 4 * place + zi - away + 32
    lag = seed_from // 4 - place

    def chip(z_, core_):
        return device(core_=core_, place_=(z_ // 4) % 8, zi_=z_ % 4)

    sibling = device(core_=1 - core)
    up, down = device(place_=(place + 1) % 8), device(place_=(place + 7) % 8)

    load = pltpu.make_async_copy(density, raw, raw_sem.at[0])
    load.start()
    barrier = pltpu.get_barrier_semaphore()
    friends = [sibling, up, down]
    for step in range(1, 4):
        friends.append(device(y_=(y + step) % 4))
        for other in range(2):
            friends.append(device(zi_=(zi + step) % 4, core_=other))
            friends.append(device(x_=(x + step) % 4, core_=other))
    for friend in friends:
        pl.semaphore_signal(barrier, inc=1, device_id=friend, device_id_type=MESH)

    @pl.when(x != 0)
    def _():
        for other in range(2):
            pl.semaphore_signal(barrier, inc=1, device_id=chip(seed_to, other), device_id_type=MESH)
            pl.semaphore_signal(barrier, inc=1, device_id=chip(seed_from, other), device_id_type=MESH)

    pattern = occupancy[...].astype(F32).astype(BF16)
    blocks = pattern.shape[0]

    def mask(row0, rows, col0, cols):
        row_block = (row0 + lax.broadcasted_iota(jnp.int32, (rows, blocks), 0)) // BS
        rows_hot = (row_block == lax.broadcasted_iota(jnp.int32, (rows, blocks), 1)).astype(F32).astype(BF16)
        col_block = (col0 + lax.broadcasted_iota(jnp.int32, (blocks, cols), 1)) // BS
        cols_hot = (col_block == lax.broadcasted_iota(jnp.int32, (blocks, cols), 0)).astype(F32).astype(BF16)
        chosen = jnp.dot(rows_hot, pattern, preferred_element_type=F32).astype(BF16)
        return jnp.dot(chosen, cols_hot, preferred_element_type=F32)

    occupied = mask(384 * row, 384, 768 * col, 768).astype(BF16)
    load.wait()
    tile[...] = raw[...] * occupied
    pl.semaphore_wait(barrier, len(friends) + jnp.where(x == 0, 0, 4))

    pending = []

    def send(src, dst, send_sem, recv_sem, target, here=None, only=None):
        copy = pltpu.make_async_remote_copy(
            src_ref=src, dst_ref=dst, send_sem=send_sem, recv_sem=recv_sem, device_id=target, device_id_type=MESH
        )
        if here is None:
            go = only
        else:
            go = jnp.logical_not(here) if only is None else jnp.logical_and(only, jnp.logical_not(here))

            @pl.when(here if only is None else jnp.logical_and(only, here))
            def _():
                pltpu.make_async_copy(src, dst, recv_sem).start()

        if go is None:
            copy.start()
        else:
            pl.when(go)(copy.start)
        pending.append((copy, go))

    def settle(most):
        for copy, go in pending[:most]:
            if go is None:
                copy.wait_send()
            else:
                pl.when(go)(copy.wait_send)
        del pending[:most]

    def arrive(dst, recv_sem):
        pltpu.make_async_remote_copy(
            src_ref=dst, dst_ref=dst, send_sem=recv_sem, recv_sem=recv_sem, device_id=sibling, device_id_type=MESH
        ).wait_recv()

    seed_zi = seed_to % 4

    def seeds(c):
        for other in range(2):
            send(
                tile.at[pl.ds(192 * other, 192), pl.ds(pl.multiple_of(384 * (seed_zi % 2) + BS * c, BS), BS)],
                right1.at[c, pl.ds(pl.multiple_of(384 * group + 192 * other, 64), 192)],
                seed_s.at[2 * c + other], seed_r.at[c], chip(seed_to, other),
                here=jnp.logical_and(x == 0, core == other), only=core == seed_zi // 2,
            )

    def left_group():
        for h in range(2):
            to_zi = (2 * core + h + 4 - x) % 4
            send(
                tile.at[pl.ds(pl.multiple_of(192 * zh, 64), 192), pl.ds(384 * h, 384)],
                left.at[y, pl.ds(pl.multiple_of(192 * (zi % 2), 64), 192)],
                a1_s.at[h], a1_r.at[zi % 2], device(zi_=to_zi, core_=zi // 2),
                here=jnp.logical_and(to_zi == zi, zi // 2 == core),
            )

    def left_open():
        for h in range(2):
            arrive(left.at[y, pl.ds(192 * h, 192)], a1_r.at[h])
        for way in range(2):
            send(left.at[y], left.at[y], a2_s.at[way], a2_r.at[way], device(y_=(y + (3 if way else 1)) % 4))

    def left_hop():
        for way in range(2):
            came = (y + (1 if way else 3)) % 4
            arrive(left.at[came], a2_r.at[way])
            ref = left.at[came, pl.ds(192 * way, 192)]
            send(ref, ref, a2_s.at[2 + way], a2_r.at[2 + way], device(y_=(y + (3 if way else 1)) % 4))

    def left_close():
        for way in range(2):
            arrive(left.at[(y + 2) % 4, pl.ds(192 * way, 192)], a2_r.at[2 + way])

    hops = (2, 4)

    def span(q, way, hop, core_, narrow):
        at = (place + (8 - hop if way == 0 else hop)) % 8
        if q == 0:
            start, size = 384 * ((at + lag) % 4) + 192 * core_, 192
        else:
            start, size = 384 * (at % 4) + 192 * (at // 4) + 96 * core_, 96
        if narrow:
            size //= 2
            start = start + size * way
        return pl.ds(pl.multiple_of(start, 16), size)

    def ring_number(q, c, way, hop):
        return 4 * NC * q + (2 * c + way) * hops[q] + hop - 1

    def share_number(q, c, way, hop):
        return 5 * NC * q + (2 * hops[q] + 1) * c + (0 if hop == 0 else 1 + way * hops[q] + hop - 1)

    def ring_send(q, c, way, hop):
        ref = rights[q].at[c, span(q, way, hop - 1, core, hop == hops[q])]
        n = ring_number(q, c, way, hop)
        send(ref, ref, ring_s.at[n], ring_r.at[n], down if way else up)

    def share(q, c, way, hop):
        ref = rights[q].at[c, span(q, way, hop, core, hop == hops[q])]
        n = share_number(q, c, way, hop)
        send(ref, ref, sib_s.at[n], sib_r.at[n], sibling)

    def ring_open(q, c):
        ring_send(q, c, 0, 1)
        ring_send(q, c, 1, 1)
        share(q, c, 0, 0)

    def ring_hop(q, c, hop):
        for way in range(2):
            arrive(rights[q].at[c, span(q, way, hop, core, hop == hops[q])], ring_r.at[ring_number(q, c, way, hop)])
            if hop < hops[q]:
                ring_send(q, c, way, hop + 1)
            share(q, c, way, hop)

    def ring_close(q, c, first=0, last=None):
        for hop in range(first, (hops[q] if last is None else last) + 1):
            for way in range(2 if hop else 1):
                arrive(rights[q].at[c, span(q, way, hop, 1 - core, hop == hops[q])], sib_r.at[share_number(q, c, way, hop)])

    def seed_open(c):
        arrive(right1.at[c, span(0, 0, 0, core, False)], seed_r.at[c])
        ring_open(0, c)

    def product(q, c):
        total = jnp.dot(left[0], rights[q][c, pl.ds(0, 384)], preferred_element_type=F32)
        for j in range(1, 4):
            total += jnp.dot(left[j], rights[q][c, pl.ds(384 * j, 384)], preferred_element_type=F32)
        return total

    def masks():
        slab_mask[...] = mask(384 * (4 * group + kind) + 192 * zh + 96 * core, 96, 1536 * y + 384 * zi, 384)
        for h in range(2):
            out_mask[h] = mask(384 * (4 * group + 2 * core + h) + 192 * zh + 48 * x, 48, 1536 * y + 384 * zi, 384)

    def square_part(c):
        part1[c] = product(0, c)
        for h in range(2):
            to_x = (2 * core + h + 4 - zi) % 4
            for other in range(2):
                send(
                    part1.at[c, pl.ds(192 * h + 96 * other, 96)], got1.at[c, x],
                    r1_s.at[4 * c + 2 * h + other], r1_r.at[4 * c + x], device(x_=to_x, core_=other),
                    here=jnp.logical_and(to_x == x, core == other),
                )

    def square_sum(c):
        for other in range(4):
            arrive(got1.at[c, other], r1_r.at[4 * c + other])
        total = (got1[c, 0] + got1[c, 1]) + (got1[c, 2] + got1[c, 3])
        rounded = (total * slab_mask[:, BS * c:BS * (c + 1)]).astype(BF16)
        right2[c, span(1, 0, 0, core, False)] = rounded
        square[:, BS * c:BS * (c + 1)] = rounded

    def square_rows():
        for h in range(2):
            send(
                square.at[pl.ds(48 * h, 48)], square_got.at[kind % 2], sq_s.at[h], sq_r.at[kind % 2],
                device(x_=2 * core + h, core_=kind // 2),
                here=jnp.logical_and(2 * core + h == x, kind // 2 == core),
            )

    def cube_early(c):
        ring_close(1, c, 0, 3)
        total = None
        for step in range(1, 4):
            j = (group + step) % 4
            rows = right2[c, pl.ds(pl.multiple_of(384 * j, 128), 384)]
            term = jnp.dot(left[j], rows, preferred_element_type=F32)
            total = term if total is None else total + term
        early[c] = total

    def cube_part(c):
        ring_close(1, c, 4)
        rows = right2[c, pl.ds(pl.multiple_of(384 * group, 128), 384)]
        total = early[c] + jnp.dot(left[group], rows, preferred_element_type=F32)
        for h in range(2):
            for k in range(4):
                part2[c, k, h] = total[192 * h + 48 * k:192 * h + 48 * (k + 1)]
        for step in range(1, 4):
            to_x = (x + step) % 4
            send(part2.at[c, to_x], got2.at[c, step - 1], r2_s.at[3 * c + step - 1], r2_r.at[3 * c + step - 1],
                 device(x_=to_x))

    def cube_sum(c):
        for step in range(1, 4):
            arrive(got2.at[c, step - 1], r2_r.at[3 * c + step - 1])
        for h in range(2):
            total = (part2[c, x, h] + got2[c, 0, h]) + (got2[c, 1, h] + got2[c, 2, h])
            cube = total * out_mask[h, :, BS * c:BS * (c + 1)]
            final[c, h] = 3.0 * square_got[h, :, BS * c:BS * (c + 1)].astype(F32) - 2.0 * cube
            send(
                final.at[c, h], final_got.at[c, zi % 2], f_s.at[2 * c + h], f_r.at[2 * c + zi % 2],
                device(zi_=2 * core + h, core_=zi // 2),
                here=jnp.logical_and(2 * core + h == zi, zi // 2 == core),
            )

    def finish(c):
        for e in range(2):
            arrive(final_got.at[c, e], f_r.at[2 * c + e])
            out[:, 384 * e + BS * c:384 * e + BS * (c + 1)] = final_got[c, e]

    left_group()
    seeds(0)
    seeds(1)
    seed_open(0)
    left_open()
    masks()
    seed_open(1)
    ring_hop(0, 0, 1)
    seeds(2)
    left_hop()
    seed_open(2)
    ring_hop(0, 0, 2)
    ring_hop(0, 1, 1)
    left_close()
    ring_close(0, 0)
    square_part(0)
    ring_hop(0, 2, 1)
    ring_hop(0, 1, 2)
    square_sum(0)
    ring_close(0, 1)
    ring_open(1, 0)
    square_part(1)
    ring_hop(0, 2, 2)
    ring_close(0, 2)
    square_part(2)
    ring_hop(1, 0, 1)
    square_sum(1)
    ring_open(1, 1)
    square_sum(2)
    ring_open(1, 2)
    square_rows()
    settle(20)
    ring_hop(1, 0, 2)
    ring_hop(1, 1, 1)
    ring_hop(1, 2, 1)
    settle(20)
    ring_hop(1, 0, 3)
    ring_hop(1, 1, 2)
    ring_hop(1, 2, 2)
    settle(20)
    ring_hop(1, 1, 3)
    cube_early(0)
    ring_hop(1, 2, 3)
    ring_hop(1, 0, 4)
    cube_early(1)
    ring_hop(1, 1, 4)
    cube_part(0)
    cube_early(2)
    ring_hop(1, 2, 4)
    cube_part(1)
    settle(20)
    cube_part(2)
    for h in range(2):
        arrive(square_got.at[h], sq_r.at[h])
    cube_sum(0)
    cube_sum(1)
    settle(20)
    cube_sum(2)
    settle(len(pending) - 6)
    finish(0)
    finish(1)
    finish(2)
    settle(len(pending))


def shards(density, occupancy):
    dma = pltpu.SemaphoreType.DMA
    return pl.pallas_call(
        kernel,
        name="purify",
        out_shape=jax.ShapeDtypeStruct((48, 768), F32),
        in_specs=[pl.BlockSpec(memory_space=pltpu.HBM), pl.BlockSpec(memory_space=pltpu.VMEM)],
        out_specs=pl.BlockSpec(memory_space=pltpu.VMEM),
        scratch_shapes=[
            pltpu.VMEM((384, 768), BF16),
            dma((1,)),
            pltpu.VMEM((384, 768), BF16),
            pltpu.VMEM((4, 384, 384), BF16),
            pltpu.VMEM((NC, 1536, BS), BF16),
            pltpu.VMEM((NC, 1536, BS), BF16),
            pltpu.VMEM((NC, 384, BS), F32),
            pltpu.VMEM((NC, 4, 96, BS), F32),
            pltpu.VMEM((96, 384), BF16),
            pltpu.VMEM((2, 48, 384), BF16),
            pltpu.VMEM((NC, 4, 2, 48, BS), F32),
            pltpu.VMEM((NC, 3, 2, 48, BS), F32),
            pltpu.VMEM((NC, 2, 48, BS), F32),
            pltpu.VMEM((NC, 2, 48, BS), F32),
            pltpu.VMEM((96, 384), F32),
            pltpu.VMEM((2, 48, 384), F32),
            pltpu.VMEM((NC, 384, BS), F32),
            dma((2,)), dma((2,)), dma((4,)), dma((4,)), dma((2 * NC,)), dma((NC,)),
            dma((12 * NC,)), dma((12 * NC,)), dma((14 * NC,)), dma((14 * NC,)),
            dma((4 * NC,)), dma((4 * NC,)), dma((2,)), dma((2,)),
            dma((3 * NC,)), dma((3 * NC,)), dma((2 * NC,)), dma((2 * NC,)),
        ],
        compiler_params=pltpu.CompilerParams(
            collective_id=0, has_side_effects=True, vmem_limit_bytes=60 * 1024 * 1024
        ),
        cost_estimate=pl.CostEstimate(flops=2 * 2 * 384 * 384 * 1536, bytes_accessed=2 * 384 * 768 + 4 * 48 * 768,
                                      transcendentals=0),
    )(density, occupancy)


def solution(mesh):
    return jax.shard_map(
        shards,
        mesh=mesh,
        in_specs=(P("row", "col"), P()),
        out_specs=P(("row", "layer"), "col"),
        check_vma=False,
    )
```

```python
import jax
import jax.numpy as jnp
from jax import lax
from jax.experimental import pallas as pl
from jax.experimental.pallas import tpu as pltpu
from jax.sharding import PartitionSpec as P

MESH = pl.DeviceIdType.MESH
BS = 128
NC = 3
F32 = jnp.float32
BF16 = jnp.bfloat16


def kernel(density, occupancy, out, tile, left, right1, right2, part1, got1, square, square_got, part2, got2,
           final, final_got, slab_mask, out_mask, early,
           a1_s, a1_r, a2_s, a2_r, seed_s, seed_r, ring_s, ring_r, sib_s, sib_r,
           r1_s, r1_r, sq_s, sq_r, r2_s, r2_r, f_s, f_r):
    row, col, layer = (lax.axis_index(name) for name in ("row", "col", "layer"))
    group, zi = row // 4, row % 4
    y, core = col // 2, col % 2
    zh, x = layer // 4, layer % 4
    place = 4 * zh + group
    kind = (x + zi) % 4
    rights = (right1, right2)

    def device(x_=x, y_=y, core_=core, place_=place, zi_=zi):
        return {"row": 4 * (place_ % 4) + zi_, "col": 2 * y_ + core_, "layer": 4 * (place_ // 4) + x_}

    sibling = device(core_=1 - core)
    up, down = device(place_=(place + 1) % 8), device(place_=(place + 7) % 8)

    barrier = pltpu.get_barrier_semaphore()
    friends = [sibling, up, down]
    for step in range(1, 4):
        friends.append(device(y_=(y + step) % 4))
        for other in range(2):
            friends.append(device(zi_=(zi + step) % 4, core_=other))
            friends.append(device(x_=(x + step) % 4, core_=other))
    for friend in friends:
        pl.semaphore_signal(barrier, inc=1, device_id=friend, device_id_type=MESH)

    pattern = occupancy[...].astype(F32).astype(BF16)
    blocks = pattern.shape[0]

    def mask(row0, rows, col0, cols):
        row_block = (row0 + lax.broadcasted_iota(jnp.int32, (rows, blocks), 0)) // BS
        rows_hot = (row_block == lax.broadcasted_iota(jnp.int32, (rows, blocks), 1)).astype(F32).astype(BF16)
        col_block = (col0 + lax.broadcasted_iota(jnp.int32, (blocks, cols), 1)) // BS
        cols_hot = (col_block == lax.broadcasted_iota(jnp.int32, (blocks, cols), 0)).astype(F32).astype(BF16)
        chosen = jnp.dot(rows_hot, pattern, preferred_element_type=F32).astype(BF16)
        return jnp.dot(chosen, cols_hot, preferred_element_type=F32)

    tile[...] = density[...] * mask(384 * row, 384, 768 * col, 768).astype(BF16)
    pl.semaphore_wait(barrier, len(friends))

    pending = []

    def send(src, dst, send_sem, recv_sem, target, here=None, only=None):
        copy = pltpu.make_async_remote_copy(
            src_ref=src, dst_ref=dst, send_sem=send_sem, recv_sem=recv_sem, device_id=target, device_id_type=MESH
        )
        if here is None:
            go = only
        else:
            go = jnp.logical_not(here) if only is None else jnp.logical_and(only, jnp.logical_not(here))

            @pl.when(here if only is None else jnp.logical_and(only, here))
            def _():
                pltpu.make_async_copy(src, dst, recv_sem).start()

        if go is None:
            copy.start()
        else:
            pl.when(go)(copy.start)
        pending.append((copy, go))

    def settle(most):
        for copy, go in pending[:most]:
            if go is None:
                copy.wait_send()
            else:
                pl.when(go)(copy.wait_send)
        del pending[:most]

    def arrive(dst, recv_sem):
        pltpu.make_async_remote_copy(
            src_ref=dst, dst_ref=dst, send_sem=recv_sem, recv_sem=recv_sem, device_id=sibling, device_id_type=MESH
        ).wait_recv()

    seed_zi = (zi + 4 - x) % 4

    def seeds(c):
        for other in range(2):
            send(
                tile.at[pl.ds(192 * other, 192), pl.ds(pl.multiple_of(384 * (seed_zi % 2) + BS * c, BS), BS)],
                right1.at[c, pl.ds(pl.multiple_of(384 * group + 192 * other, 64), 192)],
                seed_s.at[2 * c + other], seed_r.at[c], device(zi_=seed_zi, core_=other),
                here=jnp.logical_and(seed_zi == zi, core == other), only=core == seed_zi // 2,
            )

    def left_group():
        for h in range(2):
            to_zi = (2 * core + h + 4 - x) % 4
            send(
                tile.at[pl.ds(pl.multiple_of(192 * zh, 64), 192), pl.ds(384 * h, 384)],
                left.at[y, pl.ds(pl.multiple_of(192 * (zi % 2), 64), 192)],
                a1_s.at[h], a1_r.at[zi % 2], device(zi_=to_zi, core_=zi // 2),
                here=jnp.logical_and(to_zi == zi, zi // 2 == core),
            )

    def left_open():
        for h in range(2):
            arrive(left.at[y, pl.ds(192 * h, 192)], a1_r.at[h])
        for way in range(2):
            send(left.at[y], left.at[y], a2_s.at[way], a2_r.at[way], device(y_=(y + (3 if way else 1)) % 4))

    def left_hop():
        for way in range(2):
            came = (y + (1 if way else 3)) % 4
            arrive(left.at[came], a2_r.at[way])
            ref = left.at[came, pl.ds(192 * way, 192)]
            send(ref, ref, a2_s.at[2 + way], a2_r.at[2 + way], device(y_=(y + (3 if way else 1)) % 4))

    def left_close():
        for way in range(2):
            arrive(left.at[(y + 2) % 4, pl.ds(192 * way, 192)], a2_r.at[2 + way])

    hops = (2, 4)

    def span(q, way, hop, core_, narrow):
        away = (place + (8 - hop if way == 0 else hop)) % 8
        if q == 0:
            start, size = 384 * (away % 4) + 192 * core_, 192
        else:
            start, size = 384 * (away % 4) + 192 * (away // 4) + 96 * core_, 96
        if narrow:
            size //= 2
            start = start + size * way
        return pl.ds(pl.multiple_of(start, 16), size)

    def ring_number(q, c, way, hop):
        return 4 * NC * q + (2 * c + way) * hops[q] + hop - 1

    def share_number(q, c, way, hop):
        return 5 * NC * q + (2 * hops[q] + 1) * c + (0 if hop == 0 else 1 + way * hops[q] + hop - 1)

    def ring_send(q, c, way, hop):
        ref = rights[q].at[c, span(q, way, hop - 1, core, hop == hops[q])]
        n = ring_number(q, c, way, hop)
        send(ref, ref, ring_s.at[n], ring_r.at[n], down if way else up)

    def share(q, c, way, hop):
        ref = rights[q].at[c, span(q, way, hop, core, hop == hops[q])]
        n = share_number(q, c, way, hop)
        send(ref, ref, sib_s.at[n], sib_r.at[n], sibling)

    def ring_open(q, c):
        ring_send(q, c, 0, 1)
        ring_send(q, c, 1, 1)
        share(q, c, 0, 0)

    def ring_hop(q, c, hop):
        for way in range(2):
            arrive(rights[q].at[c, span(q, way, hop, core, hop == hops[q])], ring_r.at[ring_number(q, c, way, hop)])
            if hop < hops[q]:
                ring_send(q, c, way, hop + 1)
            share(q, c, way, hop)

    def ring_close(q, c, first=0, last=None):
        for hop in range(first, (hops[q] if last is None else last) + 1):
            for way in range(2 if hop else 1):
                arrive(rights[q].at[c, span(q, way, hop, 1 - core, hop == hops[q])], sib_r.at[share_number(q, c, way, hop)])

    def seed_open(c):
        arrive(right1.at[c, span(0, 0, 0, core, False)], seed_r.at[c])
        ring_open(0, c)

    def product(q, c):
        total = jnp.dot(left[0], rights[q][c, pl.ds(0, 384)], preferred_element_type=F32)
        for j in range(1, 4):
            total += jnp.dot(left[j], rights[q][c, pl.ds(384 * j, 384)], preferred_element_type=F32)
        return total

    def masks():
        slab_mask[...] = mask(384 * (4 * group + kind) + 192 * zh + 96 * core, 96, 1536 * y + 384 * zi, 384)
        for h in range(2):
            out_mask[h] = mask(384 * (4 * group + 2 * core + h) + 192 * zh + 48 * x, 48, 1536 * y + 384 * zi, 384)

    def square_part(c):
        ring_close(0, c)
        part1[c] = product(0, c)
        for h in range(2):
            to_x = (2 * core + h + 4 - zi) % 4
            for other in range(2):
                send(
                    part1.at[c, pl.ds(192 * h + 96 * other, 96)], got1.at[c, x],
                    r1_s.at[4 * c + 2 * h + other], r1_r.at[4 * c + x], device(x_=to_x, core_=other),
                    here=jnp.logical_and(to_x == x, core == other),
                )

    def square_sum(c):
        for other in range(4):
            arrive(got1.at[c, other], r1_r.at[4 * c + other])
        total = (got1[c, 0] + got1[c, 1]) + (got1[c, 2] + got1[c, 3])
        rounded = (total * slab_mask[:, BS * c:BS * (c + 1)]).astype(BF16)
        right2[c, span(1, 0, 0, core, False)] = rounded
        square[:, BS * c:BS * (c + 1)] = rounded
        ring_open(1, c)

    def square_rows():
        for h in range(2):
            send(
                square.at[pl.ds(48 * h, 48)], square_got.at[kind % 2], sq_s.at[h], sq_r.at[kind % 2],
                device(x_=2 * core + h, core_=kind // 2),
                here=jnp.logical_and(2 * core + h == x, kind // 2 == core),
            )

    def cube_early(c):
        ring_close(1, c, 0, 3)
        total = None
        for step in range(1, 4):
            j = (group + step) % 4
            rows = right2[c, pl.ds(pl.multiple_of(384 * j, 128), 384)]
            term = jnp.dot(left[j], rows, preferred_element_type=F32)
            total = term if total is None else total + term
        early[c] = total

    def cube_part(c):
        ring_close(1, c, 4)
        rows = right2[c, pl.ds(pl.multiple_of(384 * group, 128), 384)]
        total = early[c] + jnp.dot(left[group], rows, preferred_element_type=F32)
        for h in range(2):
            for k in range(4):
                part2[c, k, h] = total[192 * h + 48 * k:192 * h + 48 * (k + 1)]
        for step in range(1, 4):
            to_x = (x + step) % 4
            send(part2.at[c, to_x], got2.at[c, step - 1], r2_s.at[3 * c + step - 1], r2_r.at[3 * c + step - 1],
                 device(x_=to_x))

    def cube_sum(c):
        for step in range(1, 4):
            arrive(got2.at[c, step - 1], r2_r.at[3 * c + step - 1])
        for h in range(2):
            total = (part2[c, x, h] + got2[c, 0, h]) + (got2[c, 1, h] + got2[c, 2, h])
            cube = total * out_mask[h, :, BS * c:BS * (c + 1)]
            final[c, h] = 3.0 * square_got[h, :, BS * c:BS * (c + 1)].astype(F32) - 2.0 * cube
            send(
                final.at[c, h], final_got.at[c, zi % 2], f_s.at[2 * c + h], f_r.at[2 * c + zi % 2],
                device(zi_=2 * core + h, core_=zi // 2),
                here=jnp.logical_and(2 * core + h == zi, zi // 2 == core),
            )

    def finish(c):
        for e in range(2):
            arrive(final_got.at[c, e], f_r.at[2 * c + e])
            out[:, 384 * e + BS * c:384 * e + BS * (c + 1)] = final_got[c, e]

    seeds(0)
    left_group()
    seeds(1)
    seeds(2)
    seed_open(0)
    left_open()
    seed_open(1)
    masks()
    ring_hop(0, 0, 1)
    seed_open(2)
    left_hop()
    ring_hop(0, 0, 2)
    ring_hop(0, 1, 1)
    left_close()
    square_part(0)
    ring_hop(0, 1, 2)
    ring_hop(0, 2, 1)
    square_part(1)
    square_sum(0)
    ring_hop(0, 2, 2)
    square_part(2)
    square_sum(1)
    ring_hop(1, 0, 1)
    square_sum(2)
    square_rows()
    settle(16)
    ring_hop(1, 1, 1)
    ring_hop(1, 0, 2)
    ring_hop(1, 2, 1)
    settle(16)
    ring_hop(1, 1, 2)
    ring_hop(1, 0, 3)
    ring_hop(1, 2, 2)
    settle(16)
    ring_hop(1, 1, 3)
    cube_early(0)
    ring_hop(1, 0, 4)
    ring_hop(1, 2, 3)
    cube_early(1)
    ring_hop(1, 1, 4)
    cube_part(0)
    settle(16)
    cube_early(2)
    ring_hop(1, 2, 4)
    cube_part(1)
    cube_part(2)
    for h in range(2):
        arrive(square_got.at[h], sq_r.at[h])
    cube_sum(0)
    cube_sum(1)
    cube_sum(2)
    settle(len(pending) - 6)
    for c in range(NC):
        finish(c)
    settle(len(pending))


def shards(density, occupancy):
    dma = pltpu.SemaphoreType.DMA
    return pl.pallas_call(
        kernel,
        name="purify",
        out_shape=jax.ShapeDtypeStruct((48, 768), F32),
        in_specs=[pl.BlockSpec(memory_space=pltpu.VMEM)] * 2,
        out_specs=pl.BlockSpec(memory_space=pltpu.VMEM),
        scratch_shapes=[
            pltpu.VMEM((384, 768), BF16),
            pltpu.VMEM((4, 384, 384), BF16),
            pltpu.VMEM((NC, 1536, BS), BF16),
            pltpu.VMEM((NC, 1536, BS), BF16),
            pltpu.VMEM((NC, 384, BS), F32),
            pltpu.VMEM((NC, 4, 96, BS), F32),
            pltpu.VMEM((96, 384), BF16),
            pltpu.VMEM((2, 48, 384), BF16),
            pltpu.VMEM((NC, 4, 2, 48, BS), F32),
            pltpu.VMEM((NC, 3, 2, 48, BS), F32),
            pltpu.VMEM((NC, 2, 48, BS), F32),
            pltpu.VMEM((NC, 2, 48, BS), F32),
            pltpu.VMEM((96, 384), F32),
            pltpu.VMEM((2, 48, 384), F32),
            pltpu.VMEM((NC, 384, BS), F32),
            dma((2,)), dma((2,)), dma((4,)), dma((4,)), dma((2 * NC,)), dma((NC,)),
            dma((12 * NC,)), dma((12 * NC,)), dma((14 * NC,)), dma((14 * NC,)),
            dma((4 * NC,)), dma((4 * NC,)), dma((2,)), dma((2,)),
            dma((3 * NC,)), dma((3 * NC,)), dma((2 * NC,)), dma((2 * NC,)),
        ],
        compiler_params=pltpu.CompilerParams(
            collective_id=0, has_side_effects=True, vmem_limit_bytes=32 * 1024 * 1024
        ),
        cost_estimate=pl.CostEstimate(flops=2 * 2 * 384 * 384 * 1536, bytes_accessed=2 * 384 * 768 + 4 * 48 * 768,
                                      transcendentals=0),
    )(density, occupancy)


def solution(mesh):
    return jax.shard_map(
        shards,
        mesh=mesh,
        in_specs=(P("row", "col"), P()),
        out_specs=P(("row", "layer"), "col"),
        check_vma=False,
    )
```

```python
import jax
import jax.numpy as jnp
from jax import lax
from jax.experimental import pallas as pl
from jax.experimental.pallas import tpu as pltpu
from jax.sharding import PartitionSpec as P

MESH = pl.DeviceIdType.MESH
BS = 128
NC = 3
F32 = jnp.float32
BF16 = jnp.bfloat16


def kernel(density, occupancy, out, raw, raw_sem, tile, left, right1, right2, part1, got1, square, square_got, part2, got2,
           final, final_got, slab_mask, out_mask, early,
           a1_s, a1_r, a2_s, a2_r, seed_s, seed_r, ring_s, ring_r, sib_s, sib_r,
           r1_s, r1_r, sq_s, sq_r, r2_s, r2_r, f_s, f_r):
    row, col, layer = (lax.axis_index(name) for name in ("row", "col", "layer"))
    group, zi = row // 4, row % 4
    y, core = col // 2, col % 2
    zh, x = layer // 4, layer % 4
    place = 4 * zh + group
    kind = (x + zi) % 4
    rights = (right1, right2)

    def device(x_=x, y_=y, core_=core, place_=place, zi_=zi):
        return {"row": 4 * (place_ % 4) + zi_, "col": 2 * y_ + core_, "layer": 4 * (place_ // 4) + x_}

    twist = jnp.where(zi % 2 == 1, 2, -2)
    away = jnp.where(x == 0, 0, jnp.where(x == 1, -1, jnp.where(x == 2, twist, 1)))
    seed_to, seed_from = 4 * place + zi + away + 32, 4 * place + zi - away + 32
    lag = seed_from // 4 - place

    def chip(z_, core_):
        return device(core_=core_, place_=(z_ // 4) % 8, zi_=z_ % 4)

    sibling = device(core_=1 - core)
    up, down = device(place_=(place + 1) % 8), device(place_=(place + 7) % 8)

    load = pltpu.make_async_copy(density, raw, raw_sem.at[0])
    load.start()
    barrier = pltpu.get_barrier_semaphore()
    friends = [sibling, up, down]
    for step in range(1, 4):
        friends.append(device(y_=(y + step) % 4))
        for other in range(2):
            friends.append(device(zi_=(zi + step) % 4, core_=other))
            friends.append(device(x_=(x + step) % 4, core_=other))
    for friend in friends:
        pl.semaphore_signal(barrier, inc=1, device_id=friend, device_id_type=MESH)

    @pl.when(x != 0)
    def _():
        for other in range(2):
            pl.semaphore_signal(barrier, inc=1, device_id=chip(seed_to, other), device_id_type=MESH)
            pl.semaphore_signal(barrier, inc=1, device_id=chip(seed_from, other), device_id_type=MESH)

    pattern = occupancy[...].astype(F32).astype(BF16)
    blocks = pattern.shape[0]

    def mask(row0, rows, col0, cols):
        row_block = (row0 + lax.broadcasted_iota(jnp.int32, (rows, blocks), 0)) // BS
        rows_hot = (row_block == lax.broadcasted_iota(jnp.int32, (rows, blocks), 1)).astype(F32).astype(BF16)
        col_block = (col0 + lax.broadcasted_iota(jnp.int32, (blocks, cols), 1)) // BS
        cols_hot = (col_block == lax.broadcasted_iota(jnp.int32, (blocks, cols), 0)).astype(F32).astype(BF16)
        chosen = jnp.dot(rows_hot, pattern, preferred_element_type=F32).astype(BF16)
        return jnp.dot(chosen, cols_hot, preferred_element_type=F32)

    occupied = mask(384 * row, 384, 768 * col, 768).astype(BF16)
    load.wait()
    tile[...] = raw[...] * occupied
    pl.semaphore_wait(barrier, len(friends) + jnp.where(x == 0, 0, 4))

    pending = []

    def send(src, dst, send_sem, recv_sem, target, here=None, only=None):
        copy = pltpu.make_async_remote_copy(
            src_ref=src, dst_ref=dst, send_sem=send_sem, recv_sem=recv_sem, device_id=target, device_id_type=MESH
        )
        if here is None:
            go = only
        else:
            go = jnp.logical_not(here) if only is None else jnp.logical_and(only, jnp.logical_not(here))

            @pl.when(here if only is None else jnp.logical_and(only, here))
            def _():
                pltpu.make_async_copy(src, dst, recv_sem).start()

        if go is None:
            copy.start()
        else:
            pl.when(go)(copy.start)
        pending.append((copy, go))

    def settle(most):
        for copy, go in pending[:most]:
            if go is None:
                copy.wait_send()
            else:
                pl.when(go)(copy.wait_send)
        del pending[:most]

    def arrive(dst, recv_sem):
        pltpu.make_async_remote_copy(
            src_ref=dst, dst_ref=dst, send_sem=recv_sem, recv_sem=recv_sem, device_id=sibling, device_id_type=MESH
        ).wait_recv()

    seed_zi = seed_to % 4

    def seeds(c):
        for other in range(2):
            send(
                tile.at[pl.ds(192 * other, 192), pl.ds(pl.multiple_of(384 * (seed_zi % 2) + BS * c, BS), BS)],
                right1.at[c, pl.ds(pl.multiple_of(384 * group + 192 * other, 64), 192)],
                seed_s.at[2 * c + other], seed_r.at[c], chip(seed_to, other),
                here=jnp.logical_and(x == 0, core == other), only=core == seed_zi // 2,
            )

    def left_group():
        for h in range(2):
            to_zi = (2 * core + h + 4 - x) % 4
            send(
                tile.at[pl.ds(pl.multiple_of(192 * zh, 64), 192), pl.ds(384 * h, 384)],
                left.at[y, pl.ds(pl.multiple_of(192 * (zi % 2), 64), 192)],
                a1_s.at[h], a1_r.at[zi % 2], device(zi_=to_zi, core_=zi // 2),
                here=jnp.logical_and(to_zi == zi, zi // 2 == core),
            )

    def left_open():
        for h in range(2):
            arrive(left.at[y, pl.ds(192 * h, 192)], a1_r.at[h])
        for way in range(2):
            send(left.at[y], left.at[y], a2_s.at[way], a2_r.at[way], device(y_=(y + (3 if way else 1)) % 4))

    def left_hop():
        for way in range(2):
            came = (y + (1 if way else 3)) % 4
            arrive(left.at[came], a2_r.at[way])
            ref = left.at[came, pl.ds(192 * way, 192)]
            send(ref, ref, a2_s.at[2 + way], a2_r.at[2 + way], device(y_=(y + (3 if way else 1)) % 4))

    def left_close():
        for way in range(2):
            arrive(left.at[(y + 2) % 4, pl.ds(192 * way, 192)], a2_r.at[2 + way])

    hops = (2, 4)

    def span(q, way, hop, core_, narrow):
        at = (place + (8 - hop if way == 0 else hop)) % 8
        if q == 0:
            start, size = 384 * ((at + lag) % 4) + 192 * core_, 192
        else:
            start, size = 384 * (at % 4) + 192 * (at // 4) + 96 * core_, 96
        if narrow:
            size //= 2
            start = start + size * way
        return pl.ds(pl.multiple_of(start, 16), size)

    def ring_number(q, c, way, hop):
        return 4 * NC * q + (2 * c + way) * hops[q] + hop - 1

    def share_number(q, c, way, hop):
        return 5 * NC * q + (2 * hops[q] + 1) * c + (0 if hop == 0 else 1 + way * hops[q] + hop - 1)

    def ring_send(q, c, way, hop):
        ref = rights[q].at[c, span(q, way, hop - 1, core, hop == hops[q])]
        n = ring_number(q, c, way, hop)
        send(ref, ref, ring_s.at[n], ring_r.at[n], down if way else up)

    def share(q, c, way, hop):
        ref = rights[q].at[c, span(q, way, hop, core, hop == hops[q])]
        n = share_number(q, c, way, hop)
        send(ref, ref, sib_s.at[n], sib_r.at[n], sibling)

    def ring_open(q, c):
        ring_send(q, c, 0, 1)
        ring_send(q, c, 1, 1)
        share(q, c, 0, 0)

    def ring_hop(q, c, hop):
        for way in range(2):
            arrive(rights[q].at[c, span(q, way, hop, core, hop == hops[q])], ring_r.at[ring_number(q, c, way, hop)])
            if hop < hops[q]:
                ring_send(q, c, way, hop + 1)
            share(q, c, way, hop)

    def ring_close(q, c, first=0, last=None):
        for hop in range(first, (hops[q] if last is None else last) + 1):
            for way in range(2 if hop else 1):
                arrive(rights[q].at[c, span(q, way, hop, 1 - core, hop == hops[q])], sib_r.at[share_number(q, c, way, hop)])

    def seed_open(c):
        arrive(right1.at[c, span(0, 0, 0, core, False)], seed_r.at[c])
        ring_open(0, c)

    def product(q, c):
        total = jnp.dot(left[0], rights[q][c, pl.ds(0, 384)], preferred_element_type=F32)
        for j in range(1, 4):
            total += jnp.dot(left[j], rights[q][c, pl.ds(384 * j, 384)], preferred_element_type=F32)
        return total

    def masks():
        slab_mask[...] = mask(384 * (4 * group + kind) + 192 * zh + 96 * core, 96, 1536 * y + 384 * zi, 384)
        for h in range(2):
            out_mask[h] = mask(384 * (4 * group + 2 * core + h) + 192 * zh + 48 * x, 48, 1536 * y + 384 * zi, 384)

    def square_part(c):
        part1[c] = product(0, c)
        for h in range(2):
            to_x = (2 * core + h + 4 - zi) % 4
            for other in range(2):
                send(
                    part1.at[c, pl.ds(192 * h + 96 * other, 96)], got1.at[c, x],
                    r1_s.at[4 * c + 2 * h + other], r1_r.at[4 * c + x], device(x_=to_x, core_=other),
                    here=jnp.logical_and(to_x == x, core == other),
                )

    def square_sum(c):
        for other in range(4):
            arrive(got1.at[c, other], r1_r.at[4 * c + other])
        total = (got1[c, 0] + got1[c, 1]) + (got1[c, 2] + got1[c, 3])
        rounded = (total * slab_mask[:, BS * c:BS * (c + 1)]).astype(BF16)
        right2[c, span(1, 0, 0, core, False)] = rounded
        square[:, BS * c:BS * (c + 1)] = rounded

    def square_rows():
        for h in range(2):
            send(
                square.at[pl.ds(48 * h, 48)], square_got.at[kind % 2], sq_s.at[h], sq_r.at[kind % 2],
                device(x_=2 * core + h, core_=kind // 2),
                here=jnp.logical_and(2 * core + h == x, kind // 2 == core),
            )

    def cube_early(c):
        ring_close(1, c, 0, 3)
        total = None
        for step in range(1, 4):
            j = (group + step) % 4
            rows = right2[c, pl.ds(pl.multiple_of(384 * j, 128), 384)]
            term = jnp.dot(left[j], rows, preferred_element_type=F32)
            total = term if total is None else total + term
        early[c] = total

    def cube_part(c):
        ring_close(1, c, 4)
        rows = right2[c, pl.ds(pl.multiple_of(384 * group, 128), 384)]
        total = early[c] + jnp.dot(left[group], rows, preferred_element_type=F32)
        for h in range(2):
            for k in range(4):
                part2[c, k, h] = total[192 * h + 48 * k:192 * h + 48 * (k + 1)]
        for step in range(1, 4):
            to_x = (x + step) % 4
            send(part2.at[c, to_x], got2.at[c, step - 1], r2_s.at[3 * c + step - 1], r2_r.at[3 * c + step - 1],
                 device(x_=to_x))

    def cube_sum(c):
        for step in range(1, 4):
            arrive(got2.at[c, step - 1], r2_r.at[3 * c + step - 1])
        for h in range(2):
            total = (part2[c, x, h] + got2[c, 0, h]) + (got2[c, 1, h] + got2[c, 2, h])
            cube = total * out_mask[h, :, BS * c:BS * (c + 1)]
            final[c, h] = 3.0 * square_got[h, :, BS * c:BS * (c + 1)].astype(F32) - 2.0 * cube
            send(
                final.at[c, h], final_got.at[c, zi % 2], f_s.at[2 * c + h], f_r.at[2 * c + zi % 2],
                device(zi_=2 * core + h, core_=zi // 2),
                here=jnp.logical_and(2 * core + h == zi, zi // 2 == core),
            )

    def finish(c):
        for e in range(2):
            arrive(final_got.at[c, e], f_r.at[2 * c + e])
            out[:, 384 * e + BS * c:384 * e + BS * (c + 1)] = final_got[c, e]

    seeds(0)
    left_group()
    seeds(1)
    seeds(2)
    seed_open(0)
    left_open()
    seed_open(1)
    masks()
    ring_hop(0, 0, 1)
    seed_open(2)
    left_hop()
    ring_hop(0, 0, 2)
    ring_hop(0, 1, 1)
    left_close()
    ring_close(0, 0)
    square_part(0)
    ring_hop(0, 1, 2)
    ring_hop(0, 2, 1)
    ring_close(0, 1)
    square_part(1)
    square_sum(0)
    ring_open(1, 0)
    ring_hop(0, 2, 2)
    ring_close(0, 2)
    square_part(2)
    square_sum(1)
    ring_open(1, 1)
    ring_hop(1, 0, 1)
    square_sum(2)
    ring_open(1, 2)
    square_rows()
    settle(16)
    ring_hop(1, 1, 1)
    ring_hop(1, 0, 2)
    ring_hop(1, 2, 1)
    settle(16)
    ring_hop(1, 1, 2)
    ring_hop(1, 0, 3)
    ring_hop(1, 2, 2)
    settle(16)
    ring_hop(1, 1, 3)
    cube_early(0)
    ring_hop(1, 0, 4)
    ring_hop(1, 2, 3)
    cube_early(1)
    ring_hop(1, 1, 4)
    cube_part(0)
    settle(16)
    cube_early(2)
    ring_hop(1, 2, 4)
    cube_part(1)
    cube_part(2)
    for h in range(2):
        arrive(square_got.at[h], sq_r.at[h])
    cube_sum(0)
    cube_sum(1)
    cube_sum(2)
    settle(len(pending) - 6)
    for c in range(NC):
        finish(c)
    settle(len(pending))


def shards(density, occupancy):
    dma = pltpu.SemaphoreType.DMA
    return pl.pallas_call(
        kernel,
        name="purify",
        out_shape=jax.ShapeDtypeStruct((48, 768), F32),
        in_specs=[pl.BlockSpec(memory_space=pltpu.HBM), pl.BlockSpec(memory_space=pltpu.VMEM)],
        out_specs=pl.BlockSpec(memory_space=pltpu.VMEM),
        scratch_shapes=[
            pltpu.VMEM((384, 768), BF16),
            dma((1,)),
            pltpu.VMEM((384, 768), BF16),
            pltpu.VMEM((4, 384, 384), BF16),
            pltpu.VMEM((NC, 1536, BS), BF16),
            pltpu.VMEM((NC, 1536, BS), BF16),
            pltpu.VMEM((NC, 384, BS), F32),
            pltpu.VMEM((NC, 4, 96, BS), F32),
            pltpu.VMEM((96, 384), BF16),
            pltpu.VMEM((2, 48, 384), BF16),
            pltpu.VMEM((NC, 4, 2, 48, BS), F32),
            pltpu.VMEM((NC, 3, 2, 48, BS), F32),
            pltpu.VMEM((NC, 2, 48, BS), F32),
            pltpu.VMEM((NC, 2, 48, BS), F32),
            pltpu.VMEM((96, 384), F32),
            pltpu.VMEM((2, 48, 384), F32),
            pltpu.VMEM((NC, 384, BS), F32),
            dma((2,)), dma((2,)), dma((4,)), dma((4,)), dma((2 * NC,)), dma((NC,)),
            dma((12 * NC,)), dma((12 * NC,)), dma((14 * NC,)), dma((14 * NC,)),
            dma((4 * NC,)), dma((4 * NC,)), dma((2,)), dma((2,)),
            dma((3 * NC,)), dma((3 * NC,)), dma((2 * NC,)), dma((2 * NC,)),
        ],
        compiler_params=pltpu.CompilerParams(
            collective_id=0, has_side_effects=True, vmem_limit_bytes=60 * 1024 * 1024
        ),
        cost_estimate=pl.CostEstimate(flops=2 * 2 * 384 * 384 * 1536, bytes_accessed=2 * 384 * 768 + 4 * 48 * 768,
                                      transcendentals=0),
    )(density, occupancy)


def solution(mesh):
    return jax.shard_map(
        shards,
        mesh=mesh,
        in_specs=(P("row", "col"), P()),
        out_specs=P(("row", "layer"), "col"),
        check_vma=False,
    )
```
